512 devices in a mesh: season: 4 (over x_lo, core), gx: 8 (over y, x_hi), gy: 16 (over z).
Axes of the slice: x: 4 (x_hi: 2, x_lo: 2; x = x_hi * 2 + x_lo), y: 4, z: 16, core: 2. Of those that a mesh axis runs over, the one named last changes fastest.
Arguments:
- zone_ids: int32 [32, 64, 2048], P(None, 'gx', 'gy'), may hold values from 0 to 63
- log_perm: float32 [64], replicated, may hold values from -1 to 1
- log_disp: float32 [64], replicated, may hold values from -1 to 1
- temp_start: float32 [4, 32, 64, 2048], P('season', None, 'gx', 'gy'), may hold values from -6 to 6
- pressure_start: float32 [4, 32, 64, 2048], P('season', None, 'gx', 'gy'), may hold values from -6 to 6
- temp_observed: float32 [4, 32, 64, 2048], P('season', None, 'gx', 'gy'), may hold values from -6 to 6
- well_cells: int32 [2048], replicated, may hold values from 0 to 4194303
- well_flow: float32 [2048], replicated, may hold values from 0.5 to 2
- plan: int32 [4, 2048], P('season'), may hold values from -3 to 3
- inject_temp: float32 [4, 2048], P('season'), may hold values from -6 to 6
Outputs:
- temp_end: float32 [4, 32, 64, 2048], P('season', None, 'gx', 'gy')
- perm_sensitivity: float32 [4, 32, 64, 2048], P('season', None, 'gx', 'gy')
- zone_gradient: float32 [2, 64], replicated
The draws below stay inside these ranges and needn't reach their ends.
All inputs are finite; a program needn't handle non-finite values.
Results may differ from the reference program's by a relative error of at most 0.0003.
Values sent between devices are 32-bit elements; how exact they have to be, the bound alone decides.
No kernel may reach another device: no remote copies, remote signals or barrier semaphores. Data moves between devices by JAX's collectives and lax.ppermute only.
A program may use at most 64 MiB of HBM per device.

```python
import math
import jax
import jax.numpy as jnp

NZ = 32
ITERS = 4
NZONE = 64
NX = 64
NY = 2048
NWELL = 2048
SEASONS = 4
N_SEASON = 4


def touch_ends(drawn, own_key, least, high):
    longest = drawn.shape.index(max(drawn.shape))
    spots = []
    for shift in (0, 1):
        where = [jax.random.randint(jax.random.fold_in(own_key, axis), (), 0, length) for axis, length in enumerate(drawn.shape)]
        where[longest] = (where[longest] + shift) % drawn.shape[longest]
        spots.append(tuple(where))
    return drawn.at[spots[0]].set(least).at[spots[1]].set(high)


def steps_of(stream_key, shape, cuts, low, high):
    loudness = 1.0
    for axis_at, shards_of in cuts:
        heights = jax.random.uniform(jax.random.fold_in(jax.random.fold_in(stream_key, 6), axis_at), (shards_of,), jnp.float32, low / len(cuts), high / len(cuts))
        loudness = loudness * jnp.repeat(jnp.exp(heights), shape[axis_at] // shards_of).reshape((-1,) + (1,) * (len(shape) - 1 - axis_at))
    return loudness


def centred(stream_key, shape, scale, bound, pieces=(), kind=jnp.bfloat16):
    entries = jax.random.normal(stream_key, shape, jnp.float32) * scale
    if len(pieces) > 0:
        entries = steps_of(stream_key, shape, pieces, -0.22, 0.18) * entries
    return jnp.clip(entries, min=-bound, max=bound).astype(kind)


def setup_inputs(seed: int = 0) -> dict:
    key_of = jax.random.split(jax.random.key(seed), 11)
    return {
        "zone_ids": touch_ends(jax.random.randint(key_of[0], (NZ, NX, NY), 0, NZONE), jax.random.fold_in(key_of[0], 1), 0, NZONE - 1).astype(jnp.int32),
        "log_perm": jnp.clip(jax.random.uniform(key_of[1], (NZONE,), jnp.float32, -1.0, 1.0), -1.0, 1.0),
        "log_disp": jnp.clip(jax.random.uniform(key_of[2], (NZONE,), jnp.float32, -1.0, 1.0), -1.0, 1.0),
        "temp_start": centred(key_of[3], (SEASONS, NZ, NX, NY), 1.0, 6.0, ((0, 4), (2, 8), (3, 16)), jnp.float32),
        "pressure_start": centred(key_of[4], (SEASONS, NZ, NX, NY), 1.0, 6.0, ((0, 4), (2, 8), (3, 16)), jnp.float32),
        "temp_observed": centred(key_of[5], (SEASONS, NZ, NX, NY), 1.0, 6.0, ((0, 4), (2, 8), (3, 16)), jnp.float32),
        "well_cells": touch_ends(jax.random.randint(key_of[6], (NWELL,), 0, NZ * NX * NY), jax.random.fold_in(key_of[6], 1), 0, (NZ * NX * NY) - 1).astype(jnp.int32),
        "well_flow": jnp.clip(jnp.exp(jax.random.uniform(key_of[7], (NWELL,), jnp.float32, math.log(0.5), math.log(2.0))), 0.5, 2.0),
        "plan": touch_ends(jax.random.randint(key_of[8], (SEASONS, NWELL), -3, 4), jax.random.fold_in(key_of[8], 1), -3, 3).astype(jnp.int32),
        "inject_temp": centred(key_of[9], (SEASONS, NWELL), 1.0, 6.0, ((0, 4),), jnp.float32),
    }


STORAGE = 0.5
CONDUCT = 0.1
SMOOTH = 0.01
TIME_STEP = 0.02
HEAT_GAIN = 10.0

def pad_sides(field):
    return jnp.pad(field, ((0, 0), (1, 1), (1, 1)))

def beside_all(field):
    centre = field[:, 1:-1, 1:-1]
    stacked = jnp.pad(centre, ((1, 1), (0, 0), (0, 0)))
    sides = (field[:, :-2, 1:-1], field[:, 2:, 1:-1], field[:, 1:-1, :-2], field[:, 1:-1, 2:], stacked[:-2], stacked[2:])
    return (centre, sides)

def relax_pressure(pressure, perm, source, inside):
    press_mid, press_side = beside_all(pressure)
    perm_mid, perm_side = beside_all(perm)
    numer = source
    denom = STORAGE
    for press_other, perm_other in zip(press_side, perm_side):
        trans = 0.5 * (perm_mid + perm_other)
        numer = numer + trans * press_other
        denom = denom + trans
    return jnp.where(inside, numer / denom, 0.0)

def transport(temp, pressure, perm, disp, heating):
    temp_mid, temp_side = beside_all(temp)
    press_mid, press_side = beside_all(pressure)
    perm_mid, perm_side = beside_all(perm)
    disp_mid, disp_side = beside_all(disp)
    change = HEAT_GAIN * heating
    for index in range(6):
        trans = 0.5 * (perm_mid + perm_side[index])
        flow = trans * (press_mid - press_side[index])
        speed = jnp.sqrt(flow * flow + SMOOTH)
        spread = CONDUCT + 0.5 * (disp_mid + disp_side[index]) * speed
        flux = spread * (temp_mid - temp_side[index]) + 0.5 * flow * (temp_mid + temp_side[index])
        change = change - flux
    return temp_mid + TIME_STEP * change

def reference(zone_ids, log_perm, log_disp, temp_start, pressure_start, temp_observed, well_cells, well_flow, plan, inject_temp):
    log_perm_cells = log_perm[zone_ids]
    log_disp_cells = log_disp[zone_ids]
    inside = jnp.ones(zone_ids.shape, dtype=bool)
    layer_of = well_cells // (NX * NY)
    row_of = well_cells // NY % NX
    col_of = well_cells % NY
    flat_zones = zone_ids.reshape(-1)
    totals_perm = jnp.zeros((NZONE,), jnp.float32)
    totals_disp = jnp.zeros((NZONE,), jnp.float32)
    temps = []
    sens_list = []
    for season in range(N_SEASON):
        rate = plan[season].astype(jnp.float32) * well_flow
        warmth = jnp.maximum(rate, 0.0) * inject_temp[season]
        empty = jnp.zeros(zone_ids.shape, jnp.float32)
        source = empty.at[layer_of, row_of, col_of].add(rate)
        heating = empty.at[layer_of, row_of, col_of].add(warmth)
        press_begin = pressure_start[season]
        temp_begin = temp_start[season]

        def forward(perm_logs, disp_logs):
            perm = jnp.exp(perm_logs)
            disp = jnp.exp(disp_logs)
            pressure = press_begin
            for sweep_index in range(ITERS):
                pressure = relax_pressure(pad_sides(pressure), pad_sides(perm), source, inside)
            return transport(pad_sides(temp_begin), pad_sides(pressure), pad_sides(perm), pad_sides(disp), heating)
        temp_final, pull = jax.vjp(forward, log_perm_cells, log_disp_cells)
        grad_perm, grad_disp = pull(temp_final - temp_observed[season])
        totals_perm = totals_perm + jax.ops.segment_sum(grad_perm.reshape(-1), flat_zones, NZONE)
        totals_disp = totals_disp + jax.ops.segment_sum(grad_disp.reshape(-1), flat_zones, NZONE)
        temps.append(temp_final)
        sens_list.append(grad_perm)
    factor = (N_SEASON * NZ * NX * NY / NZONE) ** (-0.5)
    zone_gradient = jnp.stack([totals_perm, totals_disp]) * factor
    return (jnp.stack(temps), jnp.stack(sens_list), zone_gradient)
```

```python
import jax
import jax.numpy as jnp
from jax import lax
from jax.experimental import pallas as pl
from jax.experimental.pallas import tpu as pltpu
from jax.sharding import PartitionSpec as P

STORAGE = 0.5
CONDUCT = 0.1
SMOOTH = 0.01
TIME_STEP = 0.02
HEAT_GAIN = 10.0

NZ = 32
BX = 8
BY = 128
RAD = 10
WX = BX + 2 * RAD
WY = 2 * BY
OWN = RAD
SIDE = 31
FAR = 6
NWELL = 2048

VMEM = pl.BlockSpec(memory_space=pltpu.VMEM)
SMEM = pl.BlockSpec(memory_space=pltpu.SMEM)
PARAMS = pltpu.CompilerParams(vmem_limit_bytes=48 * 1024 * 1024)


def lanes(shape):
    return lax.broadcasted_iota(jnp.int32, shape, len(shape) - 1)


def rows_of(ref, x):
    return ref[pl.ds(x, NZ, stride=BX), :]


def roll(a, by, axis):
    return pltpu.roll(a, by % a.shape[axis], axis)


def edges_kernel(zone, press, temp, seen, right_o, left_o):
    lane = lanes((NZ, BY))
    for group in range(2):
        right = jnp.zeros((NZ, BY), jnp.float32)
        left = jnp.zeros((NZ, BY), jnp.float32)
        for j in range(4):
            x = 4 * group + j
            p = rows_of(press, x)
            z = (rows_of(zone, x) + 1).astype(jnp.float32)
            t = rows_of(temp, x)
            o = rows_of(seen, x)
            c = jnp.where(lane >= 118, p, roll(z, -10, 1))
            c = jnp.where(lane >= 108, c, roll(t, -20, 1))
            c = jnp.where(lane >= 102, c, roll(o, -26, 1))
            c = roll(c, -32 * j, 1)
            right = jnp.where(lane // 32 == 3 - j, c, right)
            e = jnp.where(lane < 10, p, roll(z, 10, 1))
            e = jnp.where(lane < 20, e, roll(t, 20, 1))
            e = jnp.where(lane < 26, e, roll(o, 26, 1))
            e = roll(e, 32 * j, 1)
            left = jnp.where(lane // 32 == j, e, left)
        right_o[group] = right
        left_o[group] = left


def sides_kernel(zone, press, temp, seen, left, right, up_o, down_o, up2_o, down2_o):
    for x in range(BX):
        p = rows_of(press, x)
        z = (rows_of(zone, x) + 1).astype(jnp.float32)
        t = rows_of(temp, x)
        o = rows_of(seen, x)
        up_o[x] = p
        down_o[x] = p
        up_o[8 + x] = z
        down_o[8 + x] = z
        if x >= 2:
            up_o[14 + x] = t
        if x < 6:
            down_o[16 + x] = t
        if x >= 3:
            up_o[19 + x] = o
        if x < 5:
            down_o[22 + x] = o
        if x >= 6:
            up2_o[x - 6] = p
            up2_o[x - 4] = z
        if x < 2:
            down2_o[x] = p
            down2_o[x + 2] = z
    for g in range(2):
        up_o[27 + g] = left[g]
        up_o[29 + g] = right[g]
        down_o[27 + g] = left[g]
        down_o[29 + g] = right[g]
    up2_o[4] = left[1]
    up2_o[5] = right[1]
    down2_o[4] = left[0]
    down2_o[5] = right[0]


def wells_kernel(grid_rows, grid_cols, where_ref, cells, flow, plan, inject, q_o, h_o, hit, val):
    cell = cells[...]
    layer = cell // (grid_rows * grid_cols)
    x = cell // grid_cols % grid_rows - (where_ref[0] - RAD)
    y = cell % grid_cols - where_ref[1]
    ok = (x >= 0) & (x < WX) & (y >= -RAD) & (y < BY + RAD)
    spot = jnp.where(ok, x * NZ + layer, -1)
    lane = jnp.where(y < 0, y + WY, y)
    rate = plan[...].astype(jnp.float32) * flow[...]
    warm = jnp.maximum(rate, 0.0) * inject[...]
    across = lax.broadcasted_iota(jnp.int32, (WY, NWELL), 0) == lane
    for i, field in enumerate((rate, warm)):
        high = field.astype(jnp.bfloat16).astype(jnp.float32)
        low = field - high
        val[2 * i] = jnp.where(across, high, 0.0).astype(jnp.bfloat16)
        val[2 * i + 1] = jnp.where(across, low, 0.0).astype(jnp.bfloat16)
    for part in range(4):
        size = WX * NZ // 4
        index = lax.broadcasted_iota(jnp.int32, (size, NWELL), 0) + part * size
        hit[pl.ds(part * size, size), :] = jnp.where(index == spot, 1.0, 0.0).astype(jnp.bfloat16)

    @pl.loop(0, 4)
    def _(part):
        size = WX * NZ // 4
        mine = hit[pl.ds(pl.multiple_of(part * size, 32), size), :]
        for i, out in enumerate((q_o, h_o)):
            total = jnp.zeros((size, WY), jnp.float32)
            for half in range(2):
                total = total + lax.dot_general(
                    mine,
                    val[2 * i + half],
                    (((1,), (1,)), ((), ())),
                    preferred_element_type=jnp.float32,
                )
            out[pl.ds(part * (WX // 4), WX // 4)] = total.reshape(WX // 4, NZ, WY)


def face(t, pi, pj, ti, tj, di, dj):
    dp = pi - pj
    u = t * dp
    v = u * u + SMOOTH
    inv = lax.rsqrt(v)
    speed = v * inv
    db = 0.5 * (di + dj)
    dt = ti - tj
    st = 0.5 * (ti + tj)
    flux = (CONDUCT + db * speed) * dt + u * st
    e = db * (u * inv) * dt + st
    return flux, e * t, e * dp, speed * dt


def main_kernel(
    zone, press, temp, seen, left, right, up, down, up2, down2, source, heat, table,
    temp_o, sens_o, sums_o,
    K, D, T, O, PR, TX, TY, TZ, R, M, MU, W,
    AX, AY, AZ, AB, BXX, BYY, BZZ, BBB, CXX, CYY, CZZ, CBB, SP, SD, PART,
):
    lane = lanes((NZ, BY))
    zi = lax.broadcasted_iota(jnp.int32, (NZ, WY), 0)
    top = zi == NZ - 1
    bottom = zi == 0
    perm_table = jnp.broadcast_to(table[0:1], (NZ, BY))
    disp_table = jnp.broadcast_to(table[1:2], (NZ, BY))

    def look(tab, index):
        return jnp.take_along_axis(tab, index, axis=1, mode="promise_in_bounds")

    def ahead(a):
        return roll(a, -1, 1)

    def behind(a):
        return roll(a, 1, 1)

    def above(a):
        return roll(a, -1, 0)

    def below(a):
        return roll(a, 1, 0)

    for r in range(WX):
        t = o = None
        if r < 2:
            p, z, cl, cr, j = up2[r], up2[2 + r], up2[4], up2[5], r + 6
        elif r < 10:
            j = r - 2
            p, z, cl, cr = up[j], up[8 + j], up[27 + j // 4], up[29 + j // 4]
            if j >= 2:
                t = up[14 + j]
            if j >= 3:
                o = up[19 + j]
        elif r < 18:
            j = r - 10
            p, z, cl, cr = rows_of(press, j), rows_of(zone, j) + 1, left[j // 4], right[j // 4]
            t, o = rows_of(temp, j), rows_of(seen, j)
        elif r < 26:
            j = r - 18
            p, z, cl, cr = down[j], down[8 + j], down[27 + j // 4], down[29 + j // 4]
            if j < 6:
                t = down[16 + j]
            if j < 5:
                o = down[22 + j]
        else:
            j = r - 26
            p, z, cl, cr = down2[j], down2[2 + j], down2[4], down2[5]
        cl = roll(cl, 32 * (j % 4), 1)
        cr = roll(cr, -32 * (j % 4), 1)
        PR[0, r, :, 0:BY] = p
        PR[0, r, :, BY:WY] = jnp.where(lane >= 118, cl, jnp.where(lane < 10, cr, 0.0))
        z = z.astype(jnp.int32)
        zh = jnp.where(lane >= 118, roll(cl, 10, 1), jnp.where(lane < 10, roll(cr, -10, 1), 0.0))
        zh = zh.astype(jnp.int32)
        K[r, :, 0:BY] = look(perm_table, z)
        K[r, :, BY:WY] = look(perm_table, zh)
        if 4 <= r < 24:
            D[r, :, 0:BY] = look(disp_table, z)
            D[r, :, BY:WY] = look(disp_table, zh)
            T[r, :, 0:BY] = t
            T[r, :, BY:WY] = jnp.where(lane >= 122, roll(cl, 20, 1), jnp.where(lane < 6, roll(cr, -20, 1), 0.0))
        if 5 <= r < 23:
            O[r, :, 0:BY] = o
            O[r, :, BY:WY] = jnp.where(lane >= 123, roll(cl, 26, 1), jnp.where(lane < 5, roll(cr, -26, 1), 0.0))

    TX[0] = 0.5 * (K[0] + K[1])

    def coefficients(x, carry):
        k = K[x]
        tx = 0.5 * (k + K[x + 1])
        ty = 0.5 * (k + ahead(k))
        half = 0.5 * k
        tz = jnp.where(top, 0.0, half + above(half))
        total = STORAGE + TX[x - 1] + tx + ty + behind(ty) + tz + below(tz)
        total = total + jnp.where(top | bottom, half, 0.0)
        TX[x] = tx
        TY[x] = ty
        TZ[x] = tz
        R[x] = jnp.where(k > 0.0, 1.0 / total, 0.0)
        return carry

    lax.fori_loop(1, WX - 1, coefficients, 0)

    def spread(ref, x):
        a = ref[x]
        ty, tz = TY[x], TZ[x]
        return (
            TX[x] * ref[x + 1]
            + TX[x - 1] * ref[x - 1]
            + ty * ahead(a)
            + behind(ty * a)
            + tz * above(a)
            + below(tz * a)
        )

    for s in range(1, 5):

        def sweep(x, carry, s=s):
            PR[s, x] = (source[x] + spread(PR.at[s - 1], x)) * R[x]
            return carry

        lax.fori_loop(s, WX - s, sweep, 0)

    PE = PR.at[4]

    def face_x(x):
        return face(TX[x], PE[x], PE[x + 1], T[x], T[x + 1], D[x], D[x + 1])

    def transport(keep):
        def step(x, before):
            t, p, d = T[x], PE[x], D[x]
            fx, ax, bx, cx = face_x(x)
            fy, ay, by, cy = face(TY[x], p, ahead(p), t, ahead(t), d, ahead(d))
            half = 0.5 * K[x]
            tz = TZ[x] + jnp.where(top, half, 0.0)

            def over(a):
                return jnp.where(top, 0.0, above(a))

            fz, az, bz, cz = face(tz, p, over(p), t, over(t), d, over(d))
            fb, ab, bb, cb = face(half[0:8], p[0:8], 0.0, t[0:8], 0.0, d[0:8], 0.0)
            fall = jnp.concatenate([-fb, jnp.zeros((NZ - 8, WY), jnp.float32)], axis=0)
            out = fx - before + fy - behind(fy) + fz - jnp.where(bottom, fall, below(fz))
            end = t + TIME_STEP * (HEAT_GAIN * heat[x] - out)
            M[x] = jnp.where(R[x] > 0.0, (-TIME_STEP) * (end - O[x]), 0.0)
            AX[x], AY[x], AZ[x], AB[x] = ax, ay, az, ab
            if keep:
                BXX[x], BYY[x], BZZ[x], BBB[x] = bx, by, bz, bb
                CXX[x], CYY[x], CZZ[x], CBB[x] = cx, cy, cz, cb
                SP[x - 9] = end[:, 0:BY]
            return fx

        return step

    first = face_x(4)[0]
    first = lax.fori_loop(5, 9, transport(False), first)
    first = lax.fori_loop(9, 18, transport(True), first)
    lax.fori_loop(18, 23, transport(False), first)
    for x in range(BX):
        temp_o[pl.ds(x, NZ, stride=BX), :] = SP[x + 1]

    def lift(a, b8):
        wide = jnp.concatenate([b8, jnp.zeros((NZ - 8, WY), jnp.float32)], axis=0)
        return jnp.where(bottom, wide, a)

    def pull_press(x, before):
        m = M[x]
        gx = (m - M[x + 1]) * AX[x]
        gy = (m - ahead(m)) * AY[x]
        gz = (m - jnp.where(top, 0.0, above(m))) * AZ[x]
        gb = m[0:8] * AB[x]
        lam = gx - before + gy - behind(gy) + gz + lift(-below(gz), gb)
        MU[3, x] = lam * R[x]
        return gx

    lax.fori_loop(6, 22, pull_press, (M[5] - M[6]) * AX[5])

    for s in range(3, 0, -1):

        def sweep_back(x, carry, s=s):
            MU[s - 1, x] = spread(MU.at[s], x) * R[x]
            return carry

        lax.fori_loop(10 - s, 18 + s, sweep_back, 0)

    def products(x, carry):
        total = MU[0, x] * PR[1, x]
        for s in range(1, 4):
            total = total + MU[s, x] * PR[s + 1, x]
        W[x] = total
        return carry

    lax.fori_loop(9, 19, products, 0)

    def around(ref, x):
        a = ref[x]
        return (
            ref[x - 1]
            + ref[x + 1]
            + ahead(a)
            + behind(a)
            + jnp.where(top, 0.0, above(a))
            + jnp.where(bottom, 0.0, below(a))
        )

    def sensitivities(x, carry):
        m = M[x]
        gx = m - M[x + 1]
        gw = M[x - 1] - m
        gy = m - ahead(m)
        gz = m - jnp.where(top, 0.0, above(m))
        gb = m[0:8]

        def both(fx, fy, fz, fb):
            ay = gy * fy[x]
            az = gz * fz[x]
            return gx * fx[x] + gw * fx[x - 1] + ay + behind(ay) + az + lift(below(az), gb * fb[x])

        gk = both(BXX, BYY, BZZ, BBB)
        gd = both(CXX, CYY, CZZ, CBB)
        gk = gk - 6.0 * W[x] - around(W, x)
        for s in range(4):
            gk = gk + MU[s, x] * around(PR.at[s], x) + PR[s, x] * around(MU.at[s], x)
        SP[x - OWN] = (0.5 * gk * K[x])[:, 0:BY]
        SD[x - OWN] = (0.5 * gd * D[x])[:, 0:BY]
        return carry

    lax.fori_loop(OWN, OWN + BX, sensitivities, 0)
    for x in range(BX):
        sens_o[pl.ds(x, NZ, stride=BX), :] = SP[x]

    for x in range(BX):
        O[x, :, 0:BY] = rows_of(zone, x).astype(jnp.float32)

    def of_zone(z, carry):
        zf = z.astype(jnp.float32)
        total_p = jnp.zeros((NZ, BY), jnp.float32)
        total_d = jnp.zeros((NZ, BY), jnp.float32)
        for x in range(BX):
            here = O[x, :, 0:BY] == zf
            total_p = total_p + jnp.where(here, SP[x], 0.0)
            total_d = total_d + jnp.where(here, SD[x], 0.0)
        PART[z] = jnp.sum(total_p.reshape(4, 8, BY), axis=0)
        PART[z + 64] = jnp.sum(total_d.reshape(4, 8, BY), axis=0)
        return carry

    lax.fori_loop(0, 64, of_zone, 0)
    per_lane = jnp.sum(PART[...], axis=1)
    sums_o[...] = lax.dot_general(
        jnp.ones((8, BY), jnp.float32),
        per_lane,
        (((1,), (1,)), ((), ())),
        precision=lax.Precision.HIGHEST,
        preferred_element_type=jnp.float32,
    )


def shifted(array, axis, by):
    size = lax.axis_size(axis)
    pairs = [(i, i + by) for i in range(size) if 0 <= i + by < size]
    return lax.ppermute(array, axis, pairs)


def spread_sum(array, axis):
    size = lax.axis_size(axis)
    copies = jnp.broadcast_to(array[None], (size,) + array.shape)
    return lax.all_to_all(copies, axis, 0, 0).sum(0)


def f32(*shape):
    return jax.ShapeDtypeStruct(shape, jnp.float32)


def buf(*shape):
    return pltpu.VMEM(shape, jnp.float32)


def body(zone_ids, log_perm, log_disp, temp_start, pressure_start, temp_observed, well_cells, well_flow, plan, inject_temp):
    flat = (NZ * BX, BY)
    zone = zone_ids.reshape(flat)
    press = pressure_start.reshape(flat)
    temp = temp_start.reshape(flat)
    seen = temp_observed.reshape(flat)
    grid_rows = BX * lax.axis_size("gx")
    grid_cols = BY * lax.axis_size("gy")

    to_right, to_left = pl.pallas_call(
        edges_kernel,
        out_shape=(f32(2, NZ, BY), f32(2, NZ, BY)),
        in_specs=[VMEM] * 4,
        out_specs=(VMEM, VMEM),
        compiler_params=PARAMS,
        name="edges",
    )(zone, press, temp, seen)
    left = shifted(to_right, "gy", 1)
    right = shifted(to_left, "gy", -1)

    corner = jnp.stack([lax.axis_index("gx") * BX, lax.axis_index("gy") * BY]).astype(jnp.int32)
    source, heat = pl.pallas_call(
        lambda *refs: wells_kernel(grid_rows, grid_cols, *refs),
        out_shape=(f32(WX, NZ, WY), f32(WX, NZ, WY)),
        in_specs=[SMEM] + [VMEM] * 4,
        out_specs=(VMEM, VMEM),
        scratch_shapes=[pltpu.VMEM((WX * NZ, NWELL), jnp.bfloat16), pltpu.VMEM((4, WY, NWELL), jnp.bfloat16)],
        compiler_params=PARAMS,
        cost_estimate=pl.CostEstimate(flops=2 * 896 * 2048 * 1024, bytes_accessed=2 << 20, transcendentals=0),
        name="wells",
    )(corner, well_cells[None], well_flow[None], plan, inject_temp)

    to_up, to_down, to_up2, to_down2 = pl.pallas_call(
        sides_kernel,
        out_shape=(f32(SIDE, NZ, BY), f32(SIDE, NZ, BY), f32(FAR, NZ, BY), f32(FAR, NZ, BY)),
        in_specs=[VMEM] * 6,
        out_specs=(VMEM,) * 4,
        compiler_params=PARAMS,
        name="sides",
    )(zone, press, temp, seen, left, right)
    up = shifted(to_up, "gx", 1)
    down = shifted(to_down, "gx", -1)
    up2 = shifted(to_up2, "gx", 2)
    down2 = shifted(to_down2, "gx", -2)

    table = jnp.pad(jnp.exp(jnp.stack([log_perm, log_disp])), ((0, 6), (1, BY - 65)))
    temp_end, sens, sums = pl.pallas_call(
        main_kernel,
        out_shape=(f32(*flat), f32(*flat), f32(8, BY)),
        in_specs=[VMEM] * 13,
        out_specs=(VMEM,) * 3,
        scratch_shapes=[buf(WX, NZ, WY)] * 4
        + [buf(5, WX, NZ, WY)]
        + [buf(WX, NZ, WY)] * 5
        + [buf(4, WX, NZ, WY)]
        + [buf(WX, NZ, WY)]
        + ([buf(23, NZ, WY)] * 3 + [buf(23, 8, WY)]) * 3
        + [buf(9, NZ, BY), buf(9, NZ, BY), buf(128, 8, BY)],
        compiler_params=PARAMS,
        name="aquifer",
    )(zone, press, temp, seen, left, right, up, down, up2, down2, source, heat, table)

    totals = lax.psum(sums[0:1], "season")
    totals = spread_sum(totals, "gx")
    totals = spread_sum(totals, "gy")
    cells = lax.axis_size("season") * NZ * grid_rows * grid_cols
    gradient = totals.reshape(2, 64) * (cells / 64) ** (-0.5)
    return (temp_end.reshape(temp_start.shape), sens.reshape(temp_start.shape), gradient)


def solution(mesh):
    in_specs = (
        P(None, "gx", "gy"),
        P(),
        P(),
        P("season", None, "gx", "gy"),
        P("season", None, "gx", "gy"),
        P("season", None, "gx", "gy"),
        P(),
        P(),
        P("season", None),
        P("season", None),
    )
    out_specs = (P("season", None, "gx", "gy"), P("season", None, "gx", "gy"), P())
    return jax.shard_map(body, mesh=mesh, in_specs=in_specs, out_specs=out_specs, check_vma=False)
```

```python
import jax
import jax.numpy as jnp
from jax import lax
from jax.experimental import pallas as pl
from jax.experimental.pallas import tpu as pltpu
from jax.sharding import PartitionSpec as P

STORAGE = 0.5
CONDUCT = 0.1
SMOOTH = 0.01
TIME_STEP = 0.02
HEAT_GAIN = 10.0

NZ = 32
BX = 8
BY = 128
RAD = 10
WX = BX + 2 * RAD
WY = 2 * BY
OWN = RAD
SIDE = 27
FAR = 5
PAIR = 62
PRESS, ZONE, TEMP, SEEN = (0, 10), (20, 10), (36, 6), (47, 5)
NWELL = 2048
PICK = 256

VMEM = pl.BlockSpec(memory_space=pltpu.VMEM)
SMEM = pl.BlockSpec(memory_space=pltpu.SMEM)
FULL = pltpu.CompilerParams(vmem_limit_bytes=60 * 1024 * 1024)
PARAMS = pltpu.CompilerParams(vmem_limit_bytes=48 * 1024 * 1024)


def lanes(shape):
    return lax.broadcasted_iota(jnp.int32, shape, len(shape) - 1)


def rows_of(ref, x):
    return jnp.concatenate([ref[pl.ds(x + BX * v, 8, stride=4 * BX), :] for v in range(4)], axis=0)


def put_rows(ref, x, value):
    for v in range(4):
        ref[pl.ds(x + BX * v, 8, stride=4 * BX), :] = value[8 * v : 8 * v + 8]


def roll(a, by, axis):
    return pltpu.roll(a, by % a.shape[axis], axis)


def between(lane, low, high):
    if low < 0:
        return (lane >= low + BY) | (lane < high)
    return (lane >= low) & (lane < high)


def pack_rows_kernel(zone, press, temp, seen, up_o, down_o):
    for x in range(BX):
        p = rows_of(press, x)
        z = (rows_of(zone, x) + 1).astype(jnp.float32)
        t = rows_of(temp, x)
        o = rows_of(seen, x)
        up_o[x] = p
        down_o[x] = p
        up_o[8 + x] = z
        down_o[8 + x] = z
        if x >= 2:
            up_o[14 + x] = t
        if x < 6:
            down_o[16 + x] = t
        if x >= 3:
            up_o[19 + x] = o
        if x < 5:
            down_o[22 + x] = o


def pack_columns_kernel(zone, press, temp, seen, after, right_o, left_o):
    lane = lanes((NZ, BY))
    for x in range(BX):
        p = rows_of(press, x)
        z = (rows_of(zone, x) + 1).astype(jnp.float32)
        t = rows_of(temp, x)
        o = rows_of(seen, x)
        if x % 2 == 0:
            right = left = jnp.zeros((NZ, BY), jnp.float32)
        for field, (spot, reach) in ((p, PRESS), (z, ZONE), (t, TEMP), (o, SEEN)):
            spot = spot + PAIR * (x % 2)
            moved = roll(field, spot, 1) if spot else field
            start = spot - reach if spot else BY - reach
            right = jnp.where(between(lane, start, start + reach), moved, right)
            left = jnp.where(between(lane, spot, spot + reach), moved, left)
        right_o[x // 2] = right
        left_o[x // 2] = left


def corner_kernel(zone, press, left, right, after, edge_o, up2_o, down2_o):
    for i in range(BX // 2):
        edge_o[i] = left[i] + right[i]
    for i in range(2):
        up2_o[i] = rows_of(press, BX - 2 + i)
        up2_o[2 + i] = (rows_of(zone, BX - 2 + i) + 1).astype(jnp.float32)
        down2_o[i] = rows_of(press, i)
        down2_o[2 + i] = (rows_of(zone, i) + 1).astype(jnp.float32)
    up2_o[4] = left[3] + right[3]
    down2_o[4] = left[0] + right[0]


def wells_kernel(grid_rows, grid_cols, where_ref, cells, flow, plan, inject, perm_logs, disp_logs, q_o, h_o, table_o):
    lane = lanes((1, BY))
    for i, logs in enumerate((perm_logs, disp_logs)):
        row = jnp.concatenate([jnp.exp(logs[...]), jnp.zeros((1, BY - 64), jnp.float32)], axis=1)
        table_o[i : i + 1, :] = roll(row, 1, 1)

    cell = cells[...]
    layer = cell // (grid_rows * grid_cols)
    layer = layer % 4 * 8 + layer // 4
    x = cell // grid_cols % grid_rows - (where_ref[0] - RAD)
    y = cell % grid_cols - where_ref[1]
    near = (x >= 0) & (x < WX) & (y >= -RAD) & (y < BY + RAD)
    near = jnp.where(near, 1.0, 0.0)
    rate = plan[...].astype(jnp.float32) * flow[...]
    warm = jnp.maximum(rate, 0.0) * inject[...]

    def halves(field):
        high = field.astype(jnp.bfloat16).astype(jnp.float32)
        return [high, field - high]

    place = [x.astype(jnp.float32), layer.astype(jnp.float32), jnp.where(y < 0, y + WY, y).astype(jnp.float32)]
    facts = jnp.concatenate(place + [near] + halves(rate) + halves(warm), axis=0).astype(jnp.bfloat16)

    chunks = [slice(c, c + PICK) for c in range(0, NWELL, PICK)]
    across = lax.broadcasted_iota(jnp.int32, (PICK, PICK), 1)
    down = lax.broadcasted_iota(jnp.int32, (PICK, PICK), 0)
    upto = jnp.where(down <= across, 1.0, 0.0).astype(jnp.bfloat16)
    marks = jnp.concatenate([near[:, c] for c in chunks], axis=0)
    counts = jnp.dot(marks.astype(jnp.bfloat16), upto, preferred_element_type=jnp.float32)
    before = jnp.zeros((1, 1), jnp.float32)
    number = []
    for i, c in enumerate(chunks):
        number.append(jnp.where(near[:, c] > 0.0, counts[i : i + 1] + (before - 1.0), -1.0).astype(jnp.int32))
        before = before + counts[i : i + 1, PICK - 1 : PICK]
    total = jnp.sum(near).astype(jnp.int32)

    def slab(start, first):
        picked = jnp.zeros((8, PICK), jnp.float32)
        for i, c in enumerate(chunks):
            chosen = jnp.where(down + start == number[i], 1.0, 0.0).astype(jnp.bfloat16)
            picked = picked + lax.dot_general(
                facts[:, c], chosen, (((1,), (1,)), ((), ())), preferred_element_type=jnp.float32
            )
        spot = jnp.where(picked[3:4] > 0.5, picked[0:1] * NZ + picked[1:2], -1.0).astype(jnp.int32)
        column = down == picked[2:3].astype(jnp.int32)
        for i, out in enumerate((q_o, h_o)):
            parts = [jnp.where(column, picked[4 + 2 * i + j : 5 + 2 * i + j], 0.0).astype(jnp.bfloat16) for j in range(2)]
            for x0, x1 in ((1, 14), (14, 27)) if i == 0 else ((5, 14), (14, 23)):
                index = lax.broadcasted_iota(jnp.int32, ((x1 - x0) * NZ, PICK), 0) + x0 * NZ
                hit = jnp.where(index == spot, 1.0, 0.0).astype(jnp.bfloat16)
                value = jnp.zeros(((x1 - x0) * NZ, WY), jnp.float32)
                for part in parts:
                    value = value + lax.dot_general(
                        hit, part, (((1,), (1,)), ((), ())), preferred_element_type=jnp.float32
                    )
                value = value.reshape(x1 - x0, NZ, WY)
                out[x0:x1] = value if first else out[x0:x1] + value

    slab(0, True)

    @pl.loop(1, (total + (PICK - 1)) // PICK)
    def _(i):
        slab(i * PICK, False)


def face(t, pi, pj, ti, tj, di, dj):
    dp = pi - pj
    u = t * dp
    v = u * u + SMOOTH
    inv = lax.rsqrt(v)
    speed = v * inv
    db = 0.5 * (di + dj)
    dt = ti - tj
    st = 0.5 * (ti + tj)
    flux = (CONDUCT + db * speed) * dt + u * st
    e = db * (u * inv) * dt + st
    return flux, e * t, e * dp, speed * dt


def main_kernel(
    zone, press, temp, seen, edge, up, down, edge_up, edge_down, up2, down2, source, heat, table,
    temp_o, sens_o, sums_o,
    K, D, T, O, P0, P1, P2, P3, P4, TX, TY, TZ, R, M, U0, U1, U2, U3, W,
    AX, AY, AZ, AB, BXX, BYY, BZZ, BBB, CXX, CYY, CZZ, CBB, SP, SD, PART,
):
    PR = (P0, P1, P2, P3, P4)
    MU = (U0, U1, U2, U3)
    lane = lanes((NZ, BY))
    zi = lax.broadcasted_iota(jnp.int32, (NZ, WY), 0)
    top = zi == NZ - 1
    bottom = zi == 0
    perm_table = jnp.broadcast_to(table[0:1], (NZ, BY))
    disp_table = jnp.broadcast_to(table[1:2], (NZ, BY))

    def look(tab, index):
        return jnp.take_along_axis(tab, index, axis=1, mode="promise_in_bounds")

    def ahead(a):
        return roll(a, -1, 1)

    def behind(a):
        return roll(a, 1, 1)

    def above(a):
        return jnp.concatenate([a[8:], roll(a[:8], -1, 0)], axis=0)

    def below(a):
        return jnp.concatenate([roll(a[24:], 1, 0), a[:24]], axis=0)

    def halo(packed, place, j):
        spot, reach = place
        spot = spot + PAIR * (j % 2)
        moved = roll(packed, -spot, 1) if spot else packed
        return jnp.where(between(lane, -reach, reach), moved, 0.0)

    zone_lanes = between(lane, 10, 30) | between(lane, 10 + PAIR, 30 + PAIR)

    def looked(packed):
        index = jnp.where(zone_lanes, packed, 0.0).astype(jnp.int32)
        return look(perm_table, index), look(disp_table, index)

    for r in range(0, WX, 2):
        if r < 2:
            packed = up2[4]
        elif r < 10:
            packed = edge_up[(r - 2) // 2]
        elif r < 18:
            packed = edge[(r - 10) // 2]
        elif r < 26:
            packed = edge_down[(r - 18) // 2]
        else:
            packed = down2[4]
        packed_k, packed_d = looked(packed)
        for r in (r, r + 1):
            t = o = None
            if r < 2:
                p, z = up2[r], up2[2 + r]
            elif r < 10:
                j = r - 2
                p, z = up[j], up[8 + j]
                t = up[14 + j] if j >= 2 else None
                o = up[19 + j] if j >= 3 else None
            elif r < 18:
                j = r - 10
                p, z = rows_of(press, j), rows_of(zone, j) + 1
                t, o = rows_of(temp, j), rows_of(seen, j)
            elif r < 26:
                j = r - 18
                p, z = down[j], down[8 + j]
                t = down[16 + j] if j < 6 else None
                o = down[22 + j] if j < 5 else None
            else:
                j = r - 26
                p, z = down2[j], down2[2 + j]
            z = z.astype(jnp.int32)
            PR[0][r, :, 0:BY] = p
            PR[0][r, :, BY:WY] = halo(packed, PRESS, r)
            K[r, :, 0:BY] = look(perm_table, z)
            K[r, :, BY:WY] = halo(packed_k, ZONE, r)
            if 4 <= r < 24:
                D[r, :, 0:BY] = look(disp_table, z)
                D[r, :, BY:WY] = halo(packed_d, ZONE, r)
                T[r, :, 0:BY] = t
                T[r, :, BY:WY] = halo(packed, TEMP, r)
            if 5 <= r < 23:
                O[r, :, 0:BY] = o
                O[r, :, BY:WY] = halo(packed, SEEN, r)

    def coefficients(x, before):
        k = K[x]
        tx = 0.5 * (k + K[x + 1])
        ty = 0.5 * (k + ahead(k))
        half = 0.5 * k
        tz = jnp.where(top, 0.0, half + above(half))
        total = STORAGE + before + tx + ty + behind(ty) + tz + below(tz)
        total = total + jnp.where(top | bottom, half, 0.0)
        TX[x] = tx
        TY[x] = ty
        TZ[x] = tz
        R[x] = jnp.where(k > 0.0, 1.0 / total, 0.0)
        return tx

    TX[0] = 0.5 * (K[0] + K[1])
    lax.fori_loop(1, WX - 1, coefficients, 0.5 * (K[0] + K[1]), unroll=13)

    def spread(ref, x):
        a = ref[x]
        ty, tz = TY[x], TZ[x]
        return (
            TX[x] * ref[x + 1]
            + TX[x - 1] * ref[x - 1]
            + ty * ahead(a)
            + behind(ty * a)
            + tz * above(a)
            + below(tz * a)
        )

    for s in range(1, 5):

        def sweep(x, carry, s=s):
            PR[s][x] = (source[x] + spread(PR[s - 1], x)) * R[x]
            return carry

        lax.fori_loop(s, WX - s, sweep, 0, unroll=True)

    PE = PR[4]

    def face_x(x):
        return face(TX[x], PE[x], PE[x + 1], T[x], T[x + 1], D[x], D[x + 1])

    def transport(keep):
        def step(x, before):
            t, p, d = T[x], PE[x], D[x]
            fx, ax, bx, cx = face_x(x)
            fy, ay, by, cy = face(TY[x], p, ahead(p), t, ahead(t), d, ahead(d))
            half = 0.5 * K[x]
            tz = TZ[x] + jnp.where(top, half, 0.0)

            def over(a):
                return jnp.where(top, 0.0, above(a))

            fz, az, bz, cz = face(tz, p, over(p), t, over(t), d, over(d))
            fb, ab, bb, cb = face(half[0:8], p[0:8], 0.0, t[0:8], 0.0, d[0:8], 0.0)
            fall = jnp.concatenate([-fb, jnp.zeros((NZ - 8, WY), jnp.float32)], axis=0)
            out = fx - before + fy - behind(fy) + fz - jnp.where(bottom, fall, below(fz))
            end = t + TIME_STEP * (HEAT_GAIN * heat[x] - out)
            M[x] = jnp.where(R[x] > 0.0, (-TIME_STEP) * (end - O[x]), 0.0)
            AX[x], AY[x], AZ[x], AB[x] = ax, ay, az, ab
            if keep:
                BXX[x], BYY[x], BZZ[x], BBB[x] = bx, by, bz, bb
                CXX[x], CYY[x], CZZ[x], CBB[x] = cx, cy, cz, cb
                SP[x - 9] = end[:, 0:BY]
            return fx

        return step

    first = face_x(4)[0]
    first = lax.fori_loop(5, 9, transport(False), first, unroll=True)
    first = lax.fori_loop(9, 18, transport(True), first, unroll=True)
    lax.fori_loop(18, 23, transport(False), first, unroll=True)
    for x in range(BX):
        put_rows(temp_o, x, SP[x + 1])

    def lift(a, b8):
        wide = jnp.concatenate([b8, jnp.zeros((NZ - 8, WY), jnp.float32)], axis=0)
        return jnp.where(bottom, wide, a)

    def pull_press(x, before):
        m = M[x]
        gx = (m - M[x + 1]) * AX[x]
        gy = (m - ahead(m)) * AY[x]
        gz = (m - jnp.where(top, 0.0, above(m))) * AZ[x]
        gb = m[0:8] * AB[x]
        lam = gx - before + gy - behind(gy) + gz + lift(-below(gz), gb)
        MU[3][x] = lam * R[x]
        return gx

    lax.fori_loop(6, 22, pull_press, (M[5] - M[6]) * AX[5], unroll=8)

    for s in range(3, 0, -1):

        def sweep_back(x, carry, s=s):
            MU[s - 1][x] = spread(MU[s], x) * R[x]
            return carry

        lax.fori_loop(10 - s, 18 + s, sweep_back, 0, unroll=True)

    def products(x, carry):
        total = MU[0][x] * PR[1][x]
        for s in range(1, 4):
            total = total + MU[s][x] * PR[s + 1][x]
        W[x] = total
        return carry

    lax.fori_loop(9, 19, products, 0, unroll=True)

    def around(ref, x):
        a = ref[x]
        return (
            ref[x - 1]
            + ref[x + 1]
            + ahead(a)
            + behind(a)
            + jnp.where(top, 0.0, above(a))
            + jnp.where(bottom, 0.0, below(a))
        )

    def sensitivities(x, carry):
        m = M[x]
        gx = m - M[x + 1]
        gw = M[x - 1] - m
        gy = m - ahead(m)
        gz = m - jnp.where(top, 0.0, above(m))
        gb = m[0:8]

        def both(fx, fy, fz, fb):
            ay = gy * fy[x]
            az = gz * fz[x]
            return gx * fx[x] + gw * fx[x - 1] + ay + behind(ay) + az + lift(below(az), gb * fb[x])

        gk = both(BXX, BYY, BZZ, BBB)
        gd = both(CXX, CYY, CZZ, CBB)
        gk = gk - 6.0 * W[x] - around(W, x)
        for s in range(4):
            gk = gk + MU[s][x] * around(PR[s], x) + PR[s][x] * around(MU[s], x)
        SP[x - OWN] = (0.5 * gk * K[x])[:, 0:BY]
        SD[x - OWN] = (0.5 * gd * D[x])[:, 0:BY]
        return carry

    lax.fori_loop(OWN, OWN + BX, sensitivities, 0, unroll=True)
    for x in range(BX):
        put_rows(sens_o, x, SP[x])

    for x in range(BX):
        O[x, :, 0:BY] = rows_of(zone, x).astype(jnp.float32)

    def of_zone(z, carry):
        zf = z.astype(jnp.float32)
        total_p = jnp.zeros((NZ, BY), jnp.float32)
        total_d = jnp.zeros((NZ, BY), jnp.float32)
        for x in range(BX):
            here = O[x, :, 0:BY] == zf
            total_p = total_p + jnp.where(here, SP[x], 0.0)
            total_d = total_d + jnp.where(here, SD[x], 0.0)
        PART[z] = jnp.sum(total_p.reshape(4, 8, BY), axis=0)
        PART[z + 64] = jnp.sum(total_d.reshape(4, 8, BY), axis=0)
        return carry

    lax.fori_loop(0, 64, of_zone, 0, unroll=8)
    per_lane = jnp.sum(PART[...], axis=1)
    sums_o[...] = lax.dot_general(
        jnp.ones((8, BY), jnp.float32),
        per_lane,
        (((1,), (1,)), ((), ())),
        precision=lax.Precision.HIGHEST,
        preferred_element_type=jnp.float32,
    )


def shifted(array, axis, by):
    size = lax.axis_size(axis)
    pairs = [(i, i + by) for i in range(size) if 0 <= i + by < size]
    return lax.ppermute(array, axis, pairs)


def spread_sum(array, axis):
    size = lax.axis_size(axis)
    copies = jnp.broadcast_to(array[None], (size,) + array.shape)
    return lax.all_to_all(copies, axis, 0, 0).sum(0)


def f32(*shape):
    return jax.ShapeDtypeStruct(shape, jnp.float32)


def buf(*shape):
    return pltpu.VMEM(shape, jnp.float32)


def body(zone_ids, log_perm, log_disp, temp_start, pressure_start, temp_observed, well_cells, well_flow, plan, inject_temp):
    flat = (NZ * BX, BY)
    zone = zone_ids.reshape(flat)
    press = pressure_start.reshape(flat)
    temp = temp_start.reshape(flat)
    seen = temp_observed.reshape(flat)
    grid_rows = BX * lax.axis_size("gx")
    grid_cols = BY * lax.axis_size("gy")

    to_up, to_down = pl.pallas_call(
        pack_rows_kernel,
        out_shape=(f32(SIDE, NZ, BY), f32(SIDE, NZ, BY)),
        in_specs=[VMEM] * 4,
        out_specs=(VMEM,) * 2,
        compiler_params=FULL,
        name="pack_rows",
    )(zone, press, temp, seen)
    up = shifted(to_up, "gx", 1)
    down = shifted(to_down, "gx", -1)
    to_right, to_left = pl.pallas_call(
        pack_columns_kernel,
        out_shape=(f32(4, NZ, BY), f32(4, NZ, BY)),
        in_specs=[VMEM] * 4 + [pl.BlockSpec(memory_space=pl.ANY)],
        out_specs=(VMEM,) * 2,
        compiler_params=FULL,
        name="pack_columns",
    )(zone, press, temp, seen, to_up)
    left = shifted(to_right, "gy", 1)
    right = shifted(to_left, "gy", -1)
    corner = jnp.stack([lax.axis_index("gx") * BX, lax.axis_index("gy") * BY]).astype(jnp.int32)
    source, heat, table = pl.pallas_call(
        lambda *refs: wells_kernel(grid_rows, grid_cols, *refs),
        out_shape=(f32(WX, NZ, WY), f32(WX, NZ, WY), f32(8, BY)),
        in_specs=[SMEM] + [VMEM] * 6,
        out_specs=(VMEM,) * 3,
        compiler_params=PARAMS,
        cost_estimate=pl.CostEstimate(flops=1 << 28, bytes_accessed=2 << 20, transcendentals=0),
        name="wells",
    )(corner, well_cells[None], well_flow[None], plan, inject_temp, log_perm[None], log_disp[None])

    edge, to_up2, to_down2 = pl.pallas_call(
        corner_kernel,
        out_shape=(f32(4, NZ, BY), f32(FAR, NZ, BY), f32(FAR, NZ, BY)),
        in_specs=[VMEM] * 4 + [pl.BlockSpec(memory_space=pl.ANY)],
        out_specs=(VMEM,) * 3,
        compiler_params=PARAMS,
        name="corners",
    )(zone, press, left, right, table)
    edge_up = shifted(edge, "gx", 1)
    edge_down = shifted(edge, "gx", -1)
    up2 = shifted(to_up2, "gx", 2)
    down2 = shifted(to_down2, "gx", -2)

    temp_end, sens, sums = pl.pallas_call(
        main_kernel,
        out_shape=(f32(*flat), f32(*flat), f32(8, BY)),
        in_specs=[VMEM] * 14,
        out_specs=(VMEM,) * 3,
        scratch_shapes=[buf(WX, NZ, WY)] * 19
        + ([buf(23, NZ, WY)] * 3 + [buf(23, 8, WY)]) * 3
        + [buf(9, NZ, BY), buf(9, NZ, BY), buf(128, 8, BY)],
        compiler_params=PARAMS,
        name="aquifer",
    )(zone, press, temp, seen, edge, up, down, edge_up, edge_down, up2, down2, source, heat, table)

    totals = spread_sum(sums[0:1], ("season", "gx"))
    totals = spread_sum(totals, "gy")
    cells = lax.axis_size("season") * NZ * grid_rows * grid_cols
    gradient = totals.reshape(2, 64) * (cells / 64) ** (-0.5)
    return (temp_end.reshape(temp_start.shape), sens.reshape(temp_start.shape), gradient)


def solution(mesh):
    in_specs = (
        P(None, "gx", "gy"),
        P(),
        P(),
        P("season", None, "gx", "gy"),
        P("season", None, "gx", "gy"),
        P("season", None, "gx", "gy"),
        P(),
        P(),
        P("season", None),
        P("season", None),
    )
    out_specs = (P("season", None, "gx", "gy"), P("season", None, "gx", "gy"), P())
    return jax.shard_map(body, mesh=mesh, in_specs=in_specs, out_specs=out_specs, check_vma=False)
```

```python
import jax
import jax.numpy as jnp
from jax import lax
from jax.experimental import pallas as pl
from jax.experimental.pallas import tpu as pltpu
from jax.sharding import PartitionSpec as P

STORAGE = 0.5
CONDUCT = 0.1
SMOOTH = 0.01
TIME_STEP = 0.02
HEAT_GAIN = 10.0

NZ = 32
BX = 8
BY = 128
RAD = 10
WX = BX + 2 * RAD
RIM = 22
SHIFT = 52
OWN = RAD
SIDE = 27
FAR = 4
EDGE = 11
MIDDLE = range(RAD - 4, RAD + BX + 4)
OTHERS = [r for r in range(WX) if r not in MIDDLE]


def edge_place(r):
    if r in MIDDLE:
        pair, base = (r - MIDDLE[0]) // 2, 62 * (r % 2)
        return pair, {"p": (base, 10), "z": (base + 20, 10), "t": (base + 36, 6), "o": (base + 47, 5)}
    place = OTHERS.index(r)
    base = 32 * (place % 4)
    return 8 + place // 4, {"p": (base + 5, 5), "z": (base + 15, 5), "t": (base + 21, 1)}


NWELL = 2048
PICK = 256

VMEM = pl.BlockSpec(memory_space=pltpu.VMEM)
SMEM = pl.BlockSpec(memory_space=pltpu.SMEM)
FULL = pltpu.CompilerParams(vmem_limit_bytes=60 * 1024 * 1024)
PARAMS = pltpu.CompilerParams(vmem_limit_bytes=48 * 1024 * 1024)


def lanes(shape):
    return lax.broadcasted_iota(jnp.int32, shape, len(shape) - 1)


def rows_of(ref, x):
    return jnp.concatenate([ref[pl.ds(x + BX * v, 8, stride=4 * BX), :] for v in range(4)], axis=0)


def put_rows(ref, x, value):
    for v in range(4):
        ref[pl.ds(x + BX * v, 8, stride=4 * BX), :] = value[8 * v : 8 * v + 8]


def roll(a, by, axis):
    return pltpu.roll(a, by % a.shape[axis], axis)


def between(lane, low, high):
    if low < 0:
        return (lane >= low + BY) | (lane < high)
    return (lane >= low) & (lane < high)


def pack_rows_kernel(zone, press, temp, seen, up_o, down_o, up2_o, down2_o):
    for x in range(BX):
        p = rows_of(press, x)
        z = (rows_of(zone, x) + 1).astype(jnp.float32)
        t = rows_of(temp, x)
        o = rows_of(seen, x)
        up_o[x] = p
        down_o[x] = p
        up_o[8 + x] = z
        down_o[8 + x] = z
        if x >= 2:
            up_o[14 + x] = t
        if x < 6:
            down_o[16 + x] = t
        if x >= 3:
            up_o[19 + x] = o
        if x < 5:
            down_o[22 + x] = o
        if x >= 6:
            up2_o[x - 6] = p
            up2_o[x - 4] = z
        if x < 2:
            down2_o[x] = p
            down2_o[x + 2] = z


def grid_row(r, zone, press, temp, seen, up, down, up2, down2):
    row = {}
    if r < 2:
        row["p"], z = up2[r], up2[2 + r]
    elif r < 10:
        j = r - 2
        row["p"], z = up[j], up[8 + j]
        if j >= 2:
            row["t"] = up[14 + j]
        if j >= 3:
            row["o"] = up[19 + j]
    elif r < 18:
        j = r - 10
        row["p"], z = rows_of(press, j), rows_of(zone, j) + 1
        row["t"], row["o"] = rows_of(temp, j), rows_of(seen, j)
    elif r < 26:
        j = r - 18
        row["p"], z = down[j], down[8 + j]
        if j < 6:
            row["t"] = down[16 + j]
        if j < 5:
            row["o"] = down[22 + j]
    else:
        j = r - 26
        row["p"], z = down2[j], down2[2 + j]
    row["z"] = z
    return row


def pack_columns_kernel(zone, press, temp, seen, up, down, up2, down2, after, right_o, left_o):
    lane = lanes((NZ, BY))
    right, left = {}, {}
    for r in range(WX):
        row = grid_row(r, zone, press, temp, seen, up, down, up2, down2)
        index, places = edge_place(r)
        if index not in right:
            right[index] = left[index] = jnp.zeros((NZ, BY), jnp.float32)
        for name, (spot, reach) in places.items():
            if name not in row:
                continue
            field = row[name].astype(jnp.float32)
            moved = roll(field, spot, 1) if spot else field
            start = spot - reach if spot else BY - reach
            right[index] = jnp.where(between(lane, start, start + reach), moved, right[index])
            left[index] = jnp.where(between(lane, spot, spot + reach), moved, left[index])
    for index in range(EDGE):
        right_o[index] = right[index]
        left_o[index] = left[index]


def wells_kernel(grid_rows, grid_cols, where_ref, cells, flow, plan, inject, perm_logs, disp_logs, q_o, h_o, q_rim_o, h_rim_o, table_o):
    lane = lanes((1, BY))
    for i, logs in enumerate((perm_logs, disp_logs)):
        row = jnp.concatenate([jnp.exp(logs[...]), jnp.zeros((1, BY - 64), jnp.float32)], axis=1)
        table_o[i : i + 1, :] = roll(row, 1, 1)

    cell = cells[...]
    layer = cell // (grid_rows * grid_cols)
    layer = layer % 4 * 8 + layer // 4
    x = cell // grid_cols % grid_rows - (where_ref[0] - RAD)
    y = cell % grid_cols - where_ref[1]
    near = (x >= 0) & (x < WX) & (y >= -RAD) & (y < BY + RAD)
    near = jnp.where(near, 1.0, 0.0)
    rate = plan[...].astype(jnp.float32) * flow[...]
    warm = jnp.maximum(rate, 0.0) * inject[...]

    def halves(field):
        high = field.astype(jnp.bfloat16).astype(jnp.float32)
        return [high, field - high]

    place = [x.astype(jnp.float32), layer.astype(jnp.float32), (y + RAD).astype(jnp.float32)]
    facts = jnp.concatenate(place + [near] + halves(rate) + halves(warm), axis=0).astype(jnp.bfloat16)

    chunks = [slice(c, c + PICK) for c in range(0, NWELL, PICK)]
    across = lax.broadcasted_iota(jnp.int32, (PICK, PICK), 1)
    down = lax.broadcasted_iota(jnp.int32, (PICK, PICK), 0)
    upto = jnp.where(down <= across, 1.0, 0.0).astype(jnp.bfloat16)
    marks = jnp.concatenate([near[:, c] for c in chunks], axis=0)
    counts = jnp.dot(marks.astype(jnp.bfloat16), upto, preferred_element_type=jnp.float32)
    before = jnp.zeros((1, 1), jnp.float32)
    number = []
    for i, c in enumerate(chunks):
        number.append(jnp.where(near[:, c] > 0.0, counts[i : i + 1] + (before - 1.0), -1.0).astype(jnp.int32))
        before = before + counts[i : i + 1, PICK - 1 : PICK]
    total = jnp.sum(near).astype(jnp.int32)

    def slab(start, first):
        picked = jnp.zeros((8, PICK), jnp.float32)
        for i, c in enumerate(chunks):
            chosen = jnp.where(down + start == number[i], 1.0, 0.0).astype(jnp.bfloat16)
            picked = picked + lax.dot_general(
                facts[:, c], chosen, (((1,), (1,)), ((), ())), preferred_element_type=jnp.float32
            )
        px, layer, py = (picked[i : i + 1].astype(jnp.int32) for i in range(3))
        py = py - RAD
        real = picked[3:4] > 0.5
        in_middle = real & (py >= 0) & (py < BY)
        in_rim = real & ((py < RIM) | (py >= BY - RIM))
        rim_lane = jnp.where(py < 0, py + BY, jnp.where(py < RIM, py, py - SHIFT))
        for spot, column, rows, outs in (
            (jnp.where(in_middle, px * NZ + layer, -1), py, NZ, (q_o, h_o)),
            (jnp.where(in_rim, px * NZ + layer, -1), rim_lane, NZ, (q_rim_o, h_rim_o)),
        ):
            there = lax.broadcasted_iota(jnp.int32, (BY, PICK), 0) == column
            for i, out in enumerate(outs):
                parts = [jnp.where(there, picked[4 + 2 * i + j : 5 + 2 * i + j], 0.0).astype(jnp.bfloat16) for j in range(2)]
                for x0, x1 in ((1, 14), (14, 27)) if i == 0 else ((5, 14), (14, 23)):
                    index = lax.broadcasted_iota(jnp.int32, ((x1 - x0) * rows, PICK), 0) + x0 * rows
                    hit = jnp.where(index == spot, 1.0, 0.0).astype(jnp.bfloat16)
                    value = jnp.zeros(((x1 - x0) * rows, BY), jnp.float32)
                    for part in parts:
                        value = value + lax.dot_general(
                            hit, part, (((1,), (1,)), ((), ())), preferred_element_type=jnp.float32
                        )
                    value = value.reshape(x1 - x0, rows, BY)
                    out[x0:x1] = value if first else out[x0:x1] + value

    slab(0, True)

    @pl.loop(1, (total + (PICK - 1)) // PICK)
    def _(i):
        slab(i * PICK, False)


def face(t, pi, pj, ti, tj, di, dj):
    dp = pi - pj
    u = t * dp
    v = u * u + SMOOTH
    inv = lax.rsqrt(v)
    speed = v * inv
    db = 0.5 * (di + dj)
    dt = ti - tj
    st = 0.5 * (ti + tj)
    flux = (CONDUCT + db * speed) * dt + u * st
    e = db * (u * inv) * dt + st
    return flux, e * t, e * dp, speed * dt


def solve(scratch, source, heat, ends, perm_sens, disp_sens):
    (
        K, D, T, O, P0, P1, P2, P3, P4, TX, TY, TZ, R, M, U0, U1, U2, U3, W,
        AX, AY, AZ, AB, BXX, BYY, BZZ, BBB, CXX, CYY, CZZ, CBB,
    ) = scratch
    PR = (P0, P1, P2, P3, P4)
    MU = (U0, U1, U2, U3)
    at = lax.broadcasted_iota(jnp.int32, (NZ, BY), 0)
    top = at == NZ - 1
    bottom = at == 0

    def above(a):
        return jnp.concatenate([a[8:], roll(a[:8], -1, 0)], axis=0)

    def below(a):
        return jnp.concatenate([roll(a[24:], 1, 0), a[:24]], axis=0)

    def ahead(a):
        return roll(a, -1, 1)

    def behind(a):
        return roll(a, 1, 1)

    def coefficients(x, before):
        k = K[x]
        tx = 0.5 * (k + K[x + 1])
        ty = 0.5 * (k + ahead(k))
        half = 0.5 * k
        tz = jnp.where(top, 0.0, half + above(half))
        total = STORAGE + before + tx + ty + behind(ty) + tz + below(tz)
        total = total + jnp.where(top | bottom, half, 0.0)
        TX[x] = tx
        TY[x] = ty
        TZ[x] = tz
        R[x] = jnp.where(k > 0.0, 1.0 / total, 0.0)
        return tx

    TX[0] = 0.5 * (K[0] + K[1])
    lax.fori_loop(1, WX - 1, coefficients, 0.5 * (K[0] + K[1]), unroll=13)

    def spread(ref, x):
        a = ref[x]
        ty, tz = TY[x], TZ[x]
        return (
            TX[x] * ref[x + 1]
            + TX[x - 1] * ref[x - 1]
            + ty * ahead(a)
            + behind(ty * a)
            + tz * above(a)
            + below(tz * a)
        )

    for s in range(1, 5):

        def sweep(x, carry, s=s):
            PR[s][x] = (source[x] + spread(PR[s - 1], x)) * R[x]
            return carry

        lax.fori_loop(s, WX - s, sweep, 0, unroll=True)

    PE = PR[4]

    def face_x(x):
        return face(TX[x], PE[x], PE[x + 1], T[x], T[x + 1], D[x], D[x + 1])

    def transport(keep):
        def step(x, before):
            t, p, d = T[x], PE[x], D[x]
            fx, ax, bx, cx = face_x(x)
            fy, ay, by, cy = face(TY[x], p, ahead(p), t, ahead(t), d, ahead(d))
            half = 0.5 * K[x]
            tz = TZ[x] + jnp.where(top, half, 0.0)

            def over(a):
                return jnp.where(top, 0.0, above(a))

            fz, az, bz, cz = face(tz, p, over(p), t, over(t), d, over(d))
            fb, ab, bb, cb = face(half[0:8], p[0:8], 0.0, t[0:8], 0.0, d[0:8], 0.0)
            fall = jnp.concatenate([-fb, jnp.zeros((NZ - 8, BY), jnp.float32)], axis=0)
            out = fx - before + fy - behind(fy) + fz - jnp.where(bottom, fall, below(fz))
            end = t + TIME_STEP * (HEAT_GAIN * heat[x] - out)
            M[x] = jnp.where(R[x] > 0.0, (-TIME_STEP) * (end - O[x]), 0.0)
            AX[x], AY[x], AZ[x], AB[x] = ax, ay, az, ab
            if keep:
                BXX[x], BYY[x], BZZ[x], BBB[x] = bx, by, bz, bb
                CXX[x], CYY[x], CZZ[x], CBB[x] = cx, cy, cz, cb
                ends[x - 9] = end
            return fx

        return step

    first = face_x(4)[0]
    first = lax.fori_loop(5, 9, transport(False), first, unroll=True)
    first = lax.fori_loop(9, 18, transport(True), first, unroll=True)
    lax.fori_loop(18, 23, transport(False), first, unroll=True)

    def lift(a, b8):
        wide = jnp.concatenate([b8, jnp.zeros((NZ - 8, BY), jnp.float32)], axis=0)
        return jnp.where(bottom, wide, a)

    def pull_press(x, before):
        m = M[x]
        gx = (m - M[x + 1]) * AX[x]
        gy = (m - ahead(m)) * AY[x]
        gz = (m - jnp.where(top, 0.0, above(m))) * AZ[x]
        gb = m[0:8] * AB[x]
        lam = gx - before + gy - behind(gy) + gz + lift(-below(gz), gb)
        MU[3][x] = lam * R[x]
        return gx

    lax.fori_loop(6, 22, pull_press, (M[5] - M[6]) * AX[5], unroll=8)

    for s in range(3, 0, -1):

        def sweep_back(x, carry, s=s):
            MU[s - 1][x] = spread(MU[s], x) * R[x]
            return carry

        lax.fori_loop(10 - s, 18 + s, sweep_back, 0, unroll=True)

    def products(x, carry):
        total = MU[0][x] * PR[1][x]
        for s in range(1, 4):
            total = total + MU[s][x] * PR[s + 1][x]
        W[x] = total
        return carry

    lax.fori_loop(9, 19, products, 0, unroll=True)

    def around(ref, x):
        a = ref[x]
        return (
            ref[x - 1]
            + ref[x + 1]
            + ahead(a)
            + behind(a)
            + jnp.where(top, 0.0, above(a))
            + jnp.where(bottom, 0.0, below(a))
        )

    def sensitivities(x, carry):
        m = M[x]
        gx = m - M[x + 1]
        gw = M[x - 1] - m
        gy = m - ahead(m)
        gz = m - jnp.where(top, 0.0, above(m))
        gb = m[0:8]

        def both(fx, fy, fz, fb):
            ay = gy * fy[x]
            az = gz * fz[x]
            return gx * fx[x] + gw * fx[x - 1] + ay + behind(ay) + az + lift(below(az), gb * fb[x])

        gk = both(BXX, BYY, BZZ, BBB)
        gd = both(CXX, CYY, CZZ, CBB)
        gk = gk - 6.0 * W[x] - around(W, x)
        for s in range(4):
            gk = gk + MU[s][x] * around(PR[s], x) + PR[s][x] * around(MU[s], x)
        perm_sens[x - OWN] = 0.5 * gk * K[x]
        disp_sens[x - OWN] = 0.5 * gd * D[x]
        return carry

    lax.fori_loop(OWN, OWN + BX, sensitivities, 0, unroll=True)


def look(table, i, index):
    wide = jnp.broadcast_to(table[i : i + 1], index.shape)
    return jnp.take_along_axis(wide, index, axis=1, mode="promise_in_bounds")


def middle_kernel(zone, press, temp, seen, up, down, up2, down2, after, source, heat, table, ends, perm_sens, disp_sens, *scratch):
    K, D, T, O, start = scratch[:5]
    for r in range(WX):
        row = grid_row(r, zone, press, temp, seen, up, down, up2, down2)
        z = row["z"].astype(jnp.int32)
        start[r] = row["p"]
        K[r] = look(table, 0, z)
        if 4 <= r < 24:
            D[r] = look(table, 1, z)
            T[r] = row["t"]
        if 5 <= r < 23:
            O[r] = row["o"]

    solve(scratch, source, heat, ends, perm_sens, disp_sens)


def rim_kernel(
    zone, press, temp, seen, up, down, up2, down2, left, right, source, heat, table, mid_ends, mid_perm, mid_disp,
    temp_o, sens_o, sums_o, ends, perm_sens, disp_sens, SP, SD, Z, PART, temp_v, sens_v, sems, *scratch,
):
    K, D, T, O, start = scratch[:5]
    lane = lanes((NZ, BY))

    moved = (lane >= 54) & (lane < 86)
    patterns = {}

    def rims(field, packed, spot, reach):
        part = jnp.where(moved, roll(field, -SHIFT, 1), field)
        if packed is None:
            return part
        if (spot, reach) not in patterns:
            index = (jnp.where(lane < 86, lane - (BY - SHIFT), lane) + spot) & (BY - 1)
            patterns[spot, reach] = index, (lane >= BY - reach) | ((lane >= 76) & (lane < 76 + reach))
        index, here = patterns[spot, reach]
        return jnp.where(here, jnp.take_along_axis(packed, index, axis=1, mode="promise_in_bounds"), part)

    sides = {}
    for r in range(WX):
        row = grid_row(r, zone, press, temp, seen, up, down, up2, down2)
        index, places = edge_place(r)

        if index not in sides:
            sides[index] = left[index] + right[index]

        def both(name, index=index, places=places, row=row):
            return rims(row[name].astype(jnp.float32), sides[index], *places[name])

        start[r] = both("p")
        z = both("z").astype(jnp.int32)
        K[r] = look(table, 0, z)
        if 4 <= r < 24:
            D[r] = look(table, 1, z)
            T[r] = both("t")
        if 5 <= r < 23:
            O[r] = both("o") if "o" in places else rims(row["o"], None, 0, 0)

    solve(scratch, source, heat, ends, perm_sens, disp_sens)

    def joined(middle, rim):
        return jnp.where(lane < RAD, rim, jnp.where(lane >= BY - RAD, roll(rim, SHIFT, 1), middle))

    for x in range(BX):
        put_rows(temp_v, x, joined(mid_ends[x + 1], ends[x + 1]))
        SP[x] = joined(mid_perm[x], perm_sens[x])
        SD[x] = joined(mid_disp[x], disp_sens[x])
        put_rows(sens_v, x, SP[x])
        Z[x] = rows_of(zone, x).astype(jnp.float32)

    copies = [
        pltpu.make_async_copy(temp_v, temp_o, sems.at[0]),
        pltpu.make_async_copy(sens_v, sens_o, sems.at[1]),
    ]
    for copy in copies:
        copy.start()

    def of_zone(z, carry):
        zf = z.astype(jnp.float32)
        total_p = jnp.zeros((NZ, BY), jnp.float32)
        total_d = jnp.zeros((NZ, BY), jnp.float32)
        for x in range(BX):
            here = Z[x] == zf
            total_p = total_p + jnp.where(here, SP[x], 0.0)
            total_d = total_d + jnp.where(here, SD[x], 0.0)
        PART[z] = jnp.sum(total_p.reshape(4, 8, BY), axis=0)
        PART[z + 64] = jnp.sum(total_d.reshape(4, 8, BY), axis=0)
        return carry

    lax.fori_loop(0, 64, of_zone, 0, unroll=8)
    per_lane = jnp.sum(PART[...], axis=1)
    sums_o[...] = lax.dot_general(
        jnp.ones((8, BY), jnp.float32),
        per_lane,
        (((1,), (1,)), ((), ())),
        precision=lax.Precision.HIGHEST,
        preferred_element_type=jnp.float32,
    )
    for copy in copies:
        copy.wait()


def shifted(array, axis, by):
    size = lax.axis_size(axis)
    pairs = [(i, i + by) for i in range(size) if 0 <= i + by < size]
    return lax.ppermute(array, axis, pairs)


def spread_sum(array, axis):
    size = lax.axis_size(axis)
    copies = jnp.broadcast_to(array[None], (size,) + array.shape)
    return lax.all_to_all(copies, axis, 0, 0).sum(0)


def f32(*shape):
    return jax.ShapeDtypeStruct(shape, jnp.float32)


def buf(*shape):
    return pltpu.VMEM(shape, jnp.float32)


SOLVE = [buf(WX, NZ, BY)] * 19 + ([buf(23, NZ, BY)] * 3 + [buf(23, 8, BY)]) * 3


def body(zone_ids, log_perm, log_disp, temp_start, pressure_start, temp_observed, well_cells, well_flow, plan, inject_temp):
    flat = (NZ * BX, BY)
    zone = zone_ids.reshape(flat)
    press = pressure_start.reshape(flat)
    temp = temp_start.reshape(flat)
    seen = temp_observed.reshape(flat)
    grid_rows = BX * lax.axis_size("gx")
    grid_cols = BY * lax.axis_size("gy")

    to_up, to_down, to_up2, to_down2 = pl.pallas_call(
        pack_rows_kernel,
        out_shape=(f32(SIDE, NZ, BY), f32(SIDE, NZ, BY), f32(FAR, NZ, BY), f32(FAR, NZ, BY)),
        in_specs=[VMEM] * 4,
        out_specs=(VMEM,) * 4,
        compiler_params=FULL,
        name="pack_rows",
    )(zone, press, temp, seen)
    up = shifted(to_up, "gx", 1)
    down = shifted(to_down, "gx", -1)
    up2 = shifted(to_up2, "gx", 2)
    down2 = shifted(to_down2, "gx", -2)

    corner = jnp.stack([lax.axis_index("gx") * BX, lax.axis_index("gy") * BY]).astype(jnp.int32)
    source, heat, rim_source, rim_heat, table = pl.pallas_call(
        lambda *refs: wells_kernel(grid_rows, grid_cols, *refs),
        out_shape=(f32(WX, NZ, BY),) * 4 + (f32(8, BY),),
        in_specs=[SMEM] + [VMEM] * 6,
        out_specs=(VMEM,) * 5,
        compiler_params=PARAMS,
        cost_estimate=pl.CostEstimate(flops=1 << 28, bytes_accessed=2 << 20, transcendentals=0),
        name="wells",
    )(corner, well_cells[None], well_flow[None], plan, inject_temp, log_perm[None], log_disp[None])

    to_right, to_left = pl.pallas_call(
        pack_columns_kernel,
        out_shape=(f32(EDGE, NZ, BY), f32(EDGE, NZ, BY)),
        in_specs=[VMEM] * 8 + [pl.BlockSpec(memory_space=pl.ANY)],
        out_specs=(VMEM,) * 2,
        compiler_params=PARAMS,
        name="pack_columns",
    )(zone, press, temp, seen, up, down, up2, down2, table)
    left = shifted(to_right, "gy", 1)
    right = shifted(to_left, "gy", -1)

    own = (f32(9, NZ, BY), f32(BX, NZ, BY), f32(BX, NZ, BY))
    mid_ends, mid_perm, mid_disp = pl.pallas_call(
        middle_kernel,
        out_shape=own,
        in_specs=[VMEM] * 8 + [pl.BlockSpec(memory_space=pl.ANY)] + [VMEM] * 3,
        out_specs=(VMEM,) * 3,
        scratch_shapes=SOLVE,
        compiler_params=PARAMS,
        cost_estimate=pl.CostEstimate(flops=1 << 28, bytes_accessed=4 << 20, transcendentals=0),
        name="middle",
    )(zone, press, temp, seen, up, down, up2, down2, to_right, source, heat, table)
    temp_end, sens, sums = pl.pallas_call(
        rim_kernel,
        out_shape=(f32(*flat), f32(*flat), f32(8, BY)),
        in_specs=[VMEM] * 16,
        out_specs=(pl.BlockSpec(memory_space=pl.ANY), pl.BlockSpec(memory_space=pl.ANY), VMEM),
        scratch_shapes=[buf(9, NZ, BY), buf(BX, NZ, BY), buf(BX, NZ, BY)]
        + [buf(BX, NZ, BY)] * 3
        + [buf(128, 8, BY), buf(*flat), buf(*flat), pltpu.SemaphoreType.DMA((2,))]
        + SOLVE,
        compiler_params=PARAMS,
        name="rims",
    )(
        zone, press, temp, seen, up, down, up2, down2, left, right, rim_source, rim_heat, table,
        mid_ends, mid_perm, mid_disp,
    )

    totals = spread_sum(sums[0:1], ("season", "gx"))
    totals = spread_sum(totals, "gy")
    cells = lax.axis_size("season") * NZ * grid_rows * grid_cols
    gradient = totals.reshape(2, 64) * (cells / 64) ** (-0.5)
    return (temp_end.reshape(temp_start.shape), sens.reshape(temp_start.shape), gradient)


def solution(mesh):
    in_specs = (
        P(None, "gx", "gy"),
        P(),
        P(),
        P("season", None, "gx", "gy"),
        P("season", None, "gx", "gy"),
        P("season", None, "gx", "gy"),
        P(),
        P(),
        P("season", None),
        P("season", None),
    )
    out_specs = (P("season", None, "gx", "gy"), P("season", None, "gx", "gy"), P())
    return jax.shard_map(body, mesh=mesh, in_specs=in_specs, out_specs=out_specs, check_vma=False)
```

```python
import jax
import jax.numpy as jnp
from jax import lax
from jax.experimental import pallas as pl
from jax.experimental.pallas import tpu as pltpu
from jax.sharding import PartitionSpec as P

STORAGE = 0.5
CONDUCT = 0.1
SMOOTH = 0.01
TIME_STEP = 0.02
HEAT_GAIN = 10.0

NZ = 32
BX = 8
BY = 128
RAD = 10
WX = BX + 2 * RAD
RIM = 22
SHIFT = 52
OWN = RAD
SIDE = 27
FAR = 4
EDGE = 11
MIDDLE = range(RAD - 4, RAD + BX + 4)
OTHERS = [r for r in range(WX) if r not in MIDDLE]


def edge_place(r):
    if r in MIDDLE:
        pair, base = (r - MIDDLE[0]) // 2, 62 * (r % 2)
        return pair, {"p": (base, 10), "z": (base + 20, 10), "t": (base + 36, 6), "o": (base + 47, 5)}
    place = OTHERS.index(r)
    base = 32 * (place % 4)
    return 8 + place // 4, {"p": (base + 5, 5), "z": (base + 15, 5), "t": (base + 21, 1)}


NWELL = 2048
PICK = 256

VMEM = pl.BlockSpec(memory_space=pltpu.VMEM)
SMEM = pl.BlockSpec(memory_space=pltpu.SMEM)
FULL = pltpu.CompilerParams(vmem_limit_bytes=60 * 1024 * 1024)
PARAMS = pltpu.CompilerParams(vmem_limit_bytes=48 * 1024 * 1024)


def lanes(shape):
    return lax.broadcasted_iota(jnp.int32, shape, len(shape) - 1)


def rows_of(ref, x):
    return jnp.concatenate([ref[pl.ds(x + BX * v, 8, stride=4 * BX), :] for v in range(4)], axis=0)


def put_rows(ref, x, value):
    for v in range(4):
        ref[pl.ds(x + BX * v, 8, stride=4 * BX), :] = value[8 * v : 8 * v + 8]


def roll(a, by, axis):
    return pltpu.roll(a, by % a.shape[axis], axis)


def between(lane, low, high):
    if low < 0:
        return (lane >= low + BY) | (lane < high)
    return (lane >= low) & (lane < high)


def pack_rows_kernel(zone, press, temp, seen, up_o, down_o, up2_o, down2_o):
    for x in range(BX):
        p = rows_of(press, x)
        z = (rows_of(zone, x) + 1).astype(jnp.float32)
        t = rows_of(temp, x)
        o = rows_of(seen, x)
        up_o[x] = p
        down_o[x] = p
        up_o[8 + x] = z
        down_o[8 + x] = z
        if x >= 2:
            up_o[14 + x] = t
        if x < 6:
            down_o[16 + x] = t
        if x >= 3:
            up_o[19 + x] = o
        if x < 5:
            down_o[22 + x] = o
        if x >= 6:
            up2_o[x - 6] = p
            up2_o[x - 4] = z
        if x < 2:
            down2_o[x] = p
            down2_o[x + 2] = z


def grid_row(r, zone, press, temp, seen, up, down, up2, down2):
    row = {}
    if r < 2:
        row["p"], z = up2[r], up2[2 + r]
    elif r < 10:
        j = r - 2
        row["p"], z = up[j], up[8 + j]
        if j >= 2:
            row["t"] = up[14 + j]
        if j >= 3:
            row["o"] = up[19 + j]
    elif r < 18:
        j = r - 10
        row["p"], z = rows_of(press, j), rows_of(zone, j) + 1
        row["t"], row["o"] = rows_of(temp, j), rows_of(seen, j)
    elif r < 26:
        j = r - 18
        row["p"], z = down[j], down[8 + j]
        if j < 6:
            row["t"] = down[16 + j]
        if j < 5:
            row["o"] = down[22 + j]
    else:
        j = r - 26
        row["p"], z = down2[j], down2[2 + j]
    row["z"] = z
    return row


def pack_columns_kernel(zone, press, temp, seen, up, down, up2, down2, after, right_o, left_o):
    lane = lanes((NZ, BY))
    right, left = {}, {}
    for r in range(WX):
        row = grid_row(r, zone, press, temp, seen, up, down, up2, down2)
        index, places = edge_place(r)
        if index not in right:
            right[index] = left[index] = jnp.zeros((NZ, BY), jnp.float32)
        for name, (spot, reach) in places.items():
            if name not in row:
                continue
            field = row[name].astype(jnp.float32)
            moved = roll(field, spot, 1) if spot else field
            start = spot - reach if spot else BY - reach
            right[index] = jnp.where(between(lane, start, start + reach), moved, right[index])
            left[index] = jnp.where(between(lane, spot, spot + reach), moved, left[index])
    for index in range(EDGE):
        right_o[index] = right[index]
        left_o[index] = left[index]


def wells_kernel(grid_rows, grid_cols, where_ref, cells, flow, plan, inject, perm_logs, disp_logs, q_o, h_o, q_rim_o, h_rim_o, table_o):
    lane = lanes((1, BY))
    for i, logs in enumerate((perm_logs, disp_logs)):
        row = jnp.concatenate([jnp.exp(logs[...]), jnp.zeros((1, BY - 64), jnp.float32)], axis=1)
        table_o[i : i + 1, :] = roll(row, 1, 1)

    cell = cells[...]
    layer = cell // (grid_rows * grid_cols)
    layer = layer % 4 * 8 + layer // 4
    x = cell // grid_cols % grid_rows - (where_ref[0] - RAD)
    y = cell % grid_cols - where_ref[1]
    near = (x >= 0) & (x < WX) & (y >= -RAD) & (y < BY + RAD)
    near = jnp.where(near, 1.0, 0.0)
    rate = plan[...].astype(jnp.float32) * flow[...]
    warm = jnp.maximum(rate, 0.0) * inject[...]

    def halves(field):
        high = field.astype(jnp.bfloat16).astype(jnp.float32)
        return [high, field - high]

    place = [x.astype(jnp.float32), layer.astype(jnp.float32), (y + RAD).astype(jnp.float32)]
    facts = jnp.concatenate(place + [near] + halves(rate) + halves(warm), axis=0).astype(jnp.bfloat16)

    chunks = [slice(c, c + PICK) for c in range(0, NWELL, PICK)]
    across = lax.broadcasted_iota(jnp.int32, (PICK, PICK), 1)
    down = lax.broadcasted_iota(jnp.int32, (PICK, PICK), 0)
    upto = jnp.where(down <= across, 1.0, 0.0).astype(jnp.bfloat16)
    marks = jnp.concatenate([near[:, c] for c in chunks], axis=0)
    counts = jnp.dot(marks.astype(jnp.bfloat16), upto, preferred_element_type=jnp.float32)
    before = jnp.zeros((1, 1), jnp.float32)
    number = []
    for i, c in enumerate(chunks):
        number.append(jnp.where(near[:, c] > 0.0, counts[i : i + 1] + (before - 1.0), -1.0).astype(jnp.int32))
        before = before + counts[i : i + 1, PICK - 1 : PICK]
    total = jnp.sum(near).astype(jnp.int32)

    def slab(start, first):
        picked = jnp.zeros((8, PICK), jnp.float32)
        for i, c in enumerate(chunks):
            chosen = jnp.where(down + start == number[i], 1.0, 0.0).astype(jnp.bfloat16)
            picked = picked + lax.dot_general(
                facts[:, c], chosen, (((1,), (1,)), ((), ())), preferred_element_type=jnp.float32
            )
        px, layer, py = (picked[i : i + 1].astype(jnp.int32) for i in range(3))
        py = py - RAD
        real = picked[3:4] > 0.5
        in_middle = real & (py >= 0) & (py < BY)
        in_rim = real & ((py < RIM) | (py >= BY - RIM))
        rim_lane = jnp.where(py < 0, py + BY, jnp.where(py < RIM, py, py - SHIFT))
        for spot, column, rows, outs in (
            (jnp.where(in_middle, px * NZ + layer, -1), py, NZ, (q_o, h_o)),
            (jnp.where(in_rim, px * NZ + layer, -1), rim_lane, NZ, (q_rim_o, h_rim_o)),
        ):
            there = lax.broadcasted_iota(jnp.int32, (BY, PICK), 0) == column
            for i, out in enumerate(outs):
                parts = [jnp.where(there, picked[4 + 2 * i + j : 5 + 2 * i + j], 0.0).astype(jnp.bfloat16) for j in range(2)]
                for x0, x1 in ((1, 14), (14, 27)) if i == 0 else ((5, 14), (14, 23)):
                    index = lax.broadcasted_iota(jnp.int32, ((x1 - x0) * rows, PICK), 0) + x0 * rows
                    hit = jnp.where(index == spot, 1.0, 0.0).astype(jnp.bfloat16)
                    value = jnp.zeros(((x1 - x0) * rows, BY), jnp.float32)
                    for part in parts:
                        value = value + lax.dot_general(
                            hit, part, (((1,), (1,)), ((), ())), preferred_element_type=jnp.float32
                        )
                    value = value.reshape(x1 - x0, rows, BY)
                    out[x0:x1] = value if first else out[x0:x1] + value

    slab(0, True)

    @pl.loop(1, (total + (PICK - 1)) // PICK)
    def _(i):
        slab(i * PICK, False)


def face(t, pi, pj, ti, tj, di, dj):
    dp = pi - pj
    u = t * dp
    v = u * u + SMOOTH
    inv = lax.rsqrt(v)
    speed = v * inv
    db = 0.5 * (di + dj)
    dt = ti - tj
    st = 0.5 * (ti + tj)
    flux = (CONDUCT + db * speed) * dt + u * st
    e = db * (u * inv) * dt + st
    return flux, e * t, e * dp, speed * dt


def solve(scratch, source, heat, ends, perm_sens, disp_sens):
    (
        K, D, T, O, P0, P1, P2, P3, P4, TX, TY, TZ, R, M, U0, U1, U2, U3, W,
        AX, AY, AZ, AB, BXX, BYY, BZZ, BBB, CXX, CYY, CZZ, CBB,
    ) = scratch
    PR = (P0, P1, P2, P3, P4)
    MU = (U0, U1, U2, U3)
    at = lax.broadcasted_iota(jnp.int32, (NZ, BY), 0)
    top = at == NZ - 1
    bottom = at == 0

    def above(a):
        return jnp.concatenate([a[8:], roll(a[:8], -1, 0)], axis=0)

    def below(a):
        return jnp.concatenate([roll(a[24:], 1, 0), a[:24]], axis=0)

    def ahead(a):
        return roll(a, -1, 1)

    def behind(a):
        return roll(a, 1, 1)

    def coefficients(x, before):
        k = K[x]
        tx = 0.5 * (k + K[x + 1])
        ty = 0.5 * (k + ahead(k))
        half = 0.5 * k
        tz = jnp.where(top, 0.0, half + above(half))
        total = STORAGE + before + tx + ty + behind(ty) + tz + below(tz)
        total = total + jnp.where(top | bottom, half, 0.0)
        TX[x] = tx
        TY[x] = ty
        TZ[x] = tz
        R[x] = jnp.where(k > 0.0, 1.0 / total, 0.0)
        return tx

    TX[0] = 0.5 * (K[0] + K[1])
    lax.fori_loop(1, WX - 1, coefficients, 0.5 * (K[0] + K[1]), unroll=13)

    def spread(ref, x):
        a = ref[x]
        ty, tz = TY[x], TZ[x]
        return (
            TX[x] * ref[x + 1]
            + TX[x - 1] * ref[x - 1]
            + ty * ahead(a)
            + behind(ty * a)
            + tz * above(a)
            + below(tz * a)
        )

    for s in range(1, 5):

        def sweep(x, carry, s=s):
            PR[s][x] = (source[x] + spread(PR[s - 1], x)) * R[x]
            return carry

        lax.fori_loop(s, WX - s, sweep, 0, unroll=True)

    PE = PR[4]

    def face_x(x):
        return face(TX[x], PE[x], PE[x + 1], T[x], T[x + 1], D[x], D[x + 1])

    def transport(keep):
        def step(x, before):
            t, p, d = T[x], PE[x], D[x]
            fx, ax, bx, cx = face_x(x)
            fy, ay, by, cy = face(TY[x], p, ahead(p), t, ahead(t), d, ahead(d))
            half = 0.5 * K[x]
            tz = TZ[x] + jnp.where(top, half, 0.0)

            def over(a):
                return jnp.where(top, 0.0, above(a))

            fz, az, bz, cz = face(tz, p, over(p), t, over(t), d, over(d))
            fb, ab, bb, cb = face(half[0:8], p[0:8], 0.0, t[0:8], 0.0, d[0:8], 0.0)
            fall = jnp.concatenate([-fb, jnp.zeros((NZ - 8, BY), jnp.float32)], axis=0)
            out = fx - before + fy - behind(fy) + fz - jnp.where(bottom, fall, below(fz))
            end = t + TIME_STEP * (HEAT_GAIN * heat[x] - out)
            M[x] = jnp.where(R[x] > 0.0, (-TIME_STEP) * (end - O[x]), 0.0)
            AX[x], AY[x], AZ[x], AB[x] = ax, ay, az, ab
            if keep:
                BXX[x], BYY[x], BZZ[x], BBB[x] = bx, by, bz, bb
                CXX[x], CYY[x], CZZ[x], CBB[x] = cx, cy, cz, cb
                ends[x - 9] = end
            return fx

        return step

    first = face_x(4)[0]
    first = lax.fori_loop(5, 9, transport(False), first, unroll=True)
    first = lax.fori_loop(9, 18, transport(True), first, unroll=3)
    lax.fori_loop(18, 23, transport(False), first, unroll=True)

    def lift(a, b8):
        wide = jnp.concatenate([b8, jnp.zeros((NZ - 8, BY), jnp.float32)], axis=0)
        return jnp.where(bottom, wide, a)

    def pull_press(x, before):
        m = M[x]
        gx = (m - M[x + 1]) * AX[x]
        gy = (m - ahead(m)) * AY[x]
        gz = (m - jnp.where(top, 0.0, above(m))) * AZ[x]
        gb = m[0:8] * AB[x]
        lam = gx - before + gy - behind(gy) + gz + lift(-below(gz), gb)
        MU[3][x] = lam * R[x]
        return gx

    lax.fori_loop(6, 22, pull_press, (M[5] - M[6]) * AX[5], unroll=8)

    for s in range(3, 0, -1):

        def sweep_back(x, carry, s=s):
            MU[s - 1][x] = spread(MU[s], x) * R[x]
            return carry

        lax.fori_loop(10 - s, 18 + s, sweep_back, 0, unroll=True)

    def products(x, carry):
        total = MU[0][x] * PR[1][x]
        for s in range(1, 4):
            total = total + MU[s][x] * PR[s + 1][x]
        W[x] = total
        return carry

    lax.fori_loop(9, 19, products, 0, unroll=True)

    def around(ref, x):
        a = ref[x]
        return (
            ref[x - 1]
            + ref[x + 1]
            + ahead(a)
            + behind(a)
            + jnp.where(top, 0.0, above(a))
            + jnp.where(bottom, 0.0, below(a))
        )

    def sensitivities(x, carry):
        m = M[x]
        gx = m - M[x + 1]
        gw = M[x - 1] - m
        gy = m - ahead(m)
        gz = m - jnp.where(top, 0.0, above(m))
        gb = m[0:8]

        def both(fx, fy, fz, fb):
            ay = gy * fy[x]
            az = gz * fz[x]
            return gx * fx[x] + gw * fx[x - 1] + ay + behind(ay) + az + lift(below(az), gb * fb[x])

        gk = both(BXX, BYY, BZZ, BBB)
        gd = both(CXX, CYY, CZZ, CBB)
        gk = gk - 6.0 * W[x] - around(W, x)
        for s in range(4):
            gk = gk + MU[s][x] * around(PR[s], x) + PR[s][x] * around(MU[s], x)
        perm_sens[x - OWN] = 0.5 * gk * K[x]
        disp_sens[x - OWN] = 0.5 * gd * D[x]
        return carry

    lax.fori_loop(OWN, OWN + BX, sensitivities, 0, unroll=True)


def look(table, i, index):
    wide = jnp.broadcast_to(table[i : i + 1], index.shape)
    return jnp.take_along_axis(wide, index, axis=1, mode="promise_in_bounds")


def middle_kernel(zone, press, temp, seen, up, down, up2, down2, after, source, heat, table, ends, perm_sens, disp_sens, *scratch):
    K, D, T, O, start = scratch[:5]
    for r in range(WX):
        row = grid_row(r, zone, press, temp, seen, up, down, up2, down2)
        z = row["z"].astype(jnp.int32)
        start[r] = row["p"]
        K[r] = look(table, 0, z)
        if 4 <= r < 24:
            D[r] = look(table, 1, z)
            T[r] = row["t"]
        if 5 <= r < 23:
            O[r] = row["o"]

    solve(scratch, source, heat, ends, perm_sens, disp_sens)


def rim_kernel(
    zone, press, temp, seen, up, down, up2, down2, left, right, source, heat, table, mid_ends, mid_perm, mid_disp,
    temp_o, sens_o, sums_o, ends, perm_sens, disp_sens, SP, SD, Z, PART, temp_v, sens_v, sems, *scratch,
):
    K, D, T, O, start = scratch[:5]
    lane = lanes((NZ, BY))

    moved = (lane >= 54) & (lane < 86)
    patterns = {}

    def rims(field, packed, spot, reach):
        part = jnp.where(moved, roll(field, -SHIFT, 1), field)
        if packed is None:
            return part
        if (spot, reach) not in patterns:
            index = (jnp.where(lane < 86, lane - (BY - SHIFT), lane) + spot) & (BY - 1)
            patterns[spot, reach] = index, (lane >= BY - reach) | ((lane >= 76) & (lane < 76 + reach))
        index, here = patterns[spot, reach]
        return jnp.where(here, jnp.take_along_axis(packed, index, axis=1, mode="promise_in_bounds"), part)

    sides = {}
    for r in range(WX):
        row = grid_row(r, zone, press, temp, seen, up, down, up2, down2)
        index, places = edge_place(r)

        if index not in sides:
            sides[index] = left[index] + right[index]

        def both(name, index=index, places=places, row=row):
            return rims(row[name].astype(jnp.float32), sides[index], *places[name])

        start[r] = both("p")
        z = both("z").astype(jnp.int32)
        K[r] = look(table, 0, z)
        if 4 <= r < 24:
            D[r] = look(table, 1, z)
            T[r] = both("t")
        if 5 <= r < 23:
            O[r] = both("o") if "o" in places else rims(row["o"], None, 0, 0)

    solve(scratch, source, heat, ends, perm_sens, disp_sens)

    def joined(middle, rim):
        return jnp.where(lane < RAD, rim, jnp.where(lane >= BY - RAD, roll(rim, SHIFT, 1), middle))

    for x in range(BX):
        put_rows(temp_v, x, joined(mid_ends[x + 1], ends[x + 1]))
        SP[x] = joined(mid_perm[x], perm_sens[x])
        SD[x] = joined(mid_disp[x], disp_sens[x])
        put_rows(sens_v, x, SP[x])
        Z[x] = rows_of(zone, x).astype(jnp.float32)

    copies = [
        pltpu.make_async_copy(temp_v, temp_o, sems.at[0]),
        pltpu.make_async_copy(sens_v, sens_o, sems.at[1]),
    ]
    for copy in copies:
        copy.start()

    def of_zone(z, carry):
        zf = z.astype(jnp.float32)
        total_p = jnp.zeros((NZ, BY), jnp.float32)
        total_d = jnp.zeros((NZ, BY), jnp.float32)
        for x in range(BX):
            here = Z[x] == zf
            total_p = total_p + jnp.where(here, SP[x], 0.0)
            total_d = total_d + jnp.where(here, SD[x], 0.0)
        PART[z] = jnp.sum(total_p.reshape(4, 8, BY), axis=0)
        PART[z + 64] = jnp.sum(total_d.reshape(4, 8, BY), axis=0)
        return carry

    lax.fori_loop(0, 64, of_zone, 0, unroll=16)
    per_lane = jnp.sum(PART[...], axis=1)
    sums_o[...] = lax.dot_general(
        jnp.ones((8, BY), jnp.float32),
        per_lane,
        (((1,), (1,)), ((), ())),
        precision=lax.Precision.HIGHEST,
        preferred_element_type=jnp.float32,
    )
    for copy in copies:
        copy.wait()


def shifted(array, axis, by):
    size = lax.axis_size(axis)
    pairs = [(i, i + by) for i in range(size) if 0 <= i + by < size]
    return lax.ppermute(array, axis, pairs)


def spread_sum(array, axis):
    size = lax.axis_size(axis)
    copies = jnp.broadcast_to(array[None], (size,) + array.shape)
    return lax.all_to_all(copies, axis, 0, 0).sum(0)


def f32(*shape):
    return jax.ShapeDtypeStruct(shape, jnp.float32)


def buf(*shape):
    return pltpu.VMEM(shape, jnp.float32)


SOLVE = [buf(WX, NZ, BY)] * 19 + ([buf(23, NZ, BY)] * 3 + [buf(23, 8, BY)]) * 3


def body(zone_ids, log_perm, log_disp, temp_start, pressure_start, temp_observed, well_cells, well_flow, plan, inject_temp):
    flat = (NZ * BX, BY)
    zone = zone_ids.reshape(flat)
    press = pressure_start.reshape(flat)
    temp = temp_start.reshape(flat)
    seen = temp_observed.reshape(flat)
    grid_rows = BX * lax.axis_size("gx")
    grid_cols = BY * lax.axis_size("gy")

    to_up, to_down, to_up2, to_down2 = pl.pallas_call(
        pack_rows_kernel,
        out_shape=(f32(SIDE, NZ, BY), f32(SIDE, NZ, BY), f32(FAR, NZ, BY), f32(FAR, NZ, BY)),
        in_specs=[VMEM] * 4,
        out_specs=(VMEM,) * 4,
        compiler_params=FULL,
        name="pack_rows",
    )(zone, press, temp, seen)
    up = shifted(to_up, "gx", 1)
    down = shifted(to_down, "gx", -1)
    up2 = shifted(to_up2, "gx", 2)
    down2 = shifted(to_down2, "gx", -2)

    corner = jnp.stack([lax.axis_index("gx") * BX, lax.axis_index("gy") * BY]).astype(jnp.int32)
    source, heat, rim_source, rim_heat, table = pl.pallas_call(
        lambda *refs: wells_kernel(grid_rows, grid_cols, *refs),
        out_shape=(f32(WX, NZ, BY),) * 4 + (f32(8, BY),),
        in_specs=[SMEM] + [VMEM] * 6,
        out_specs=(VMEM,) * 5,
        compiler_params=PARAMS,
        cost_estimate=pl.CostEstimate(flops=1 << 28, bytes_accessed=2 << 20, transcendentals=0),
        name="wells",
    )(corner, well_cells[None], well_flow[None], plan, inject_temp, log_perm[None], log_disp[None])

    to_right, to_left = pl.pallas_call(
        pack_columns_kernel,
        out_shape=(f32(EDGE, NZ, BY), f32(EDGE, NZ, BY)),
        in_specs=[VMEM] * 8 + [pl.BlockSpec(memory_space=pl.ANY)],
        out_specs=(VMEM,) * 2,
        compiler_params=PARAMS,
        name="pack_columns",
    )(zone, press, temp, seen, up, down, up2, down2, table)
    left = shifted(to_right, "gy", 1)
    right = shifted(to_left, "gy", -1)

    own = (f32(9, NZ, BY), f32(BX, NZ, BY), f32(BX, NZ, BY))
    mid_ends, mid_perm, mid_disp = pl.pallas_call(
        middle_kernel,
        out_shape=own,
        in_specs=[VMEM] * 8 + [pl.BlockSpec(memory_space=pl.ANY)] + [VMEM] * 3,
        out_specs=(VMEM,) * 3,
        scratch_shapes=SOLVE,
        compiler_params=PARAMS,
        cost_estimate=pl.CostEstimate(flops=1 << 28, bytes_accessed=4 << 20, transcendentals=0),
        name="middle",
    )(zone, press, temp, seen, up, down, up2, down2, to_right, source, heat, table)
    temp_end, sens, sums = pl.pallas_call(
        rim_kernel,
        out_shape=(f32(*flat), f32(*flat), f32(8, BY)),
        in_specs=[VMEM] * 16,
        out_specs=(pl.BlockSpec(memory_space=pl.ANY), pl.BlockSpec(memory_space=pl.ANY), VMEM),
        scratch_shapes=[buf(9, NZ, BY), buf(BX, NZ, BY), buf(BX, NZ, BY)]
        + [buf(BX, NZ, BY)] * 3
        + [buf(128, 8, BY), buf(*flat), buf(*flat), pltpu.SemaphoreType.DMA((2,))]
        + SOLVE,
        compiler_params=PARAMS,
        name="rims",
    )(
        zone, press, temp, seen, up, down, up2, down2, left, right, rim_source, rim_heat, table,
        mid_ends, mid_perm, mid_disp,
    )

    totals = spread_sum(sums[0:1], ("season", "gx"))
    totals = spread_sum(totals, "gy")
    cells = lax.axis_size("season") * NZ * grid_rows * grid_cols
    gradient = totals.reshape(2, 64) * (cells / 64) ** (-0.5)
    return (temp_end.reshape(temp_start.shape), sens.reshape(temp_start.shape), gradient)


def solution(mesh):
    in_specs = (
        P(None, "gx", "gy"),
        P(),
        P(),
        P("season", None, "gx", "gy"),
        P("season", None, "gx", "gy"),
        P("season", None, "gx", "gy"),
        P(),
        P(),
        P("season", None),
        P("season", None),
    )
    out_specs = (P("season", None, "gx", "gy"), P("season", None, "gx", "gy"), P())
    return jax.shard_map(body, mesh=mesh, in_specs=in_specs, out_specs=out_specs, check_vma=False)
```

```python
import jax
import jax.numpy as jnp
from jax import lax
from jax.experimental import pallas as pl
from jax.experimental.pallas import tpu as pltpu
from jax.sharding import PartitionSpec as P

STORAGE = 0.5
CONDUCT = 0.1
SMOOTH = 0.01
TIME_STEP = 0.02
HEAT_GAIN = 10.0

NZ = 32
BX = 8
BY = 128
RAD = 10
WX = BX + 2 * RAD
RIM = 22
SHIFT = 52
OWN = RAD
SIDE = 27
FAR = 4
EDGE = 11
MIDDLE = range(RAD - 4, RAD + BX + 4)
OTHERS = [r for r in range(WX) if r not in MIDDLE]


def edge_place(r):
    if r in MIDDLE:
        pair, base = (r - MIDDLE[0]) // 2, 62 * (r % 2)
        return pair, {"p": (base, 10), "z": (base + 20, 10), "t": (base + 36, 6), "o": (base + 47, 5)}
    place = OTHERS.index(r)
    base = 32 * (place % 4)
    return 8 + place // 4, {"p": (base + 5, 5), "z": (base + 15, 5), "t": (base + 21, 1)}


NWELL = 2048
PICK = 256

VMEM = pl.BlockSpec(memory_space=pltpu.VMEM)
SMEM = pl.BlockSpec(memory_space=pltpu.SMEM)
FULL = pltpu.CompilerParams(vmem_limit_bytes=60 * 1024 * 1024)
PARAMS = pltpu.CompilerParams(vmem_limit_bytes=48 * 1024 * 1024)


def lanes(shape):
    return lax.broadcasted_iota(jnp.int32, shape, len(shape) - 1)


def rows_of(ref, x):
    return jnp.concatenate([ref[pl.ds(x + BX * v, 8, stride=4 * BX), :] for v in range(4)], axis=0)


def put_rows(ref, x, value):
    for v in range(4):
        ref[pl.ds(x + BX * v, 8, stride=4 * BX), :] = value[8 * v : 8 * v + 8]


def roll(a, by, axis):
    return pltpu.roll(a, by % a.shape[axis], axis)


def between(lane, low, high):
    if low < 0:
        return (lane >= low + BY) | (lane < high)
    return (lane >= low) & (lane < high)


def pack_rows_kernel(zone, press, temp, seen, up_o, down_o, up2_o, down2_o):
    for x in range(BX):
        p = rows_of(press, x)
        z = (rows_of(zone, x) + 1).astype(jnp.float32)
        t = rows_of(temp, x)
        o = rows_of(seen, x)
        up_o[x] = p
        down_o[x] = p
        up_o[8 + x] = z
        down_o[8 + x] = z
        if x >= 2:
            up_o[14 + x] = t
        if x < 6:
            down_o[16 + x] = t
        if x >= 3:
            up_o[19 + x] = o
        if x < 5:
            down_o[22 + x] = o
        if x >= 6:
            up2_o[x - 6] = p
            up2_o[x - 4] = z
        if x < 2:
            down2_o[x] = p
            down2_o[x + 2] = z


def grid_row(r, zone, press, temp, seen, up, down, up2, down2):
    row = {}
    if r < 2:
        row["p"], z = up2[r], up2[2 + r]
    elif r < 10:
        j = r - 2
        row["p"], z = up[j], up[8 + j]
        if j >= 2:
            row["t"] = up[14 + j]
        if j >= 3:
            row["o"] = up[19 + j]
    elif r < 18:
        j = r - 10
        row["p"], z = rows_of(press, j), rows_of(zone, j) + 1
        row["t"], row["o"] = rows_of(temp, j), rows_of(seen, j)
    elif r < 26:
        j = r - 18
        row["p"], z = down[j], down[8 + j]
        if j < 6:
            row["t"] = down[16 + j]
        if j < 5:
            row["o"] = down[22 + j]
    else:
        j = r - 26
        row["p"], z = down2[j], down2[2 + j]
    row["z"] = z
    return row


def pack_columns_kernel(zone, press, temp, seen, up, down, up2, down2, after, right_o, left_o):
    lane = lanes((NZ, BY))
    right, left = {}, {}
    for r in range(WX):
        row = grid_row(r, zone, press, temp, seen, up, down, up2, down2)
        index, places = edge_place(r)
        if index not in right:
            right[index] = left[index] = jnp.zeros((NZ, BY), jnp.float32)
        for name, (spot, reach) in places.items():
            if name not in row:
                continue
            field = row[name].astype(jnp.float32)
            moved = roll(field, spot, 1) if spot else field
            start = spot - reach if spot else BY - reach
            right[index] = jnp.where(between(lane, start, start + reach), moved, right[index])
            left[index] = jnp.where(between(lane, spot, spot + reach), moved, left[index])
    for index in range(EDGE):
        right_o[index] = right[index]
        left_o[index] = left[index]


def wells_kernel(grid_rows, grid_cols, where_ref, cells, flow, plan, inject, perm_logs, disp_logs, q_o, h_o, q_rim_o, h_rim_o, table_o):
    lane = lanes((1, BY))
    for i, logs in enumerate((perm_logs, disp_logs)):
        row = jnp.concatenate([jnp.exp(logs[...]), jnp.zeros((1, BY - 64), jnp.float32)], axis=1)
        table_o[i : i + 1, :] = roll(row, 1, 1)

    cell = cells[...]
    layer = cell // (grid_rows * grid_cols)
    layer = layer % 4 * 8 + layer // 4
    x = cell // grid_cols % grid_rows - (where_ref[0] - RAD)
    y = cell % grid_cols - where_ref[1]
    near = (x >= 0) & (x < WX) & (y >= -RAD) & (y < BY + RAD)
    near = jnp.where(near, 1.0, 0.0)
    rate = plan[...].astype(jnp.float32) * flow[...]
    warm = jnp.maximum(rate, 0.0) * inject[...]

    def halves(field):
        high = field.astype(jnp.bfloat16).astype(jnp.float32)
        return [high, field - high]

    place = [x.astype(jnp.float32), layer.astype(jnp.float32), (y + RAD).astype(jnp.float32)]
    facts = jnp.concatenate(place + [near] + halves(rate) + halves(warm), axis=0).astype(jnp.bfloat16)

    chunks = [slice(c, c + PICK) for c in range(0, NWELL, PICK)]
    across = lax.broadcasted_iota(jnp.int32, (PICK, PICK), 1)
    down = lax.broadcasted_iota(jnp.int32, (PICK, PICK), 0)
    upto = jnp.where(down <= across, 1.0, 0.0).astype(jnp.bfloat16)
    marks = jnp.concatenate([near[:, c] for c in chunks], axis=0)
    counts = jnp.dot(marks.astype(jnp.bfloat16), upto, preferred_element_type=jnp.float32)
    before = jnp.zeros((1, 1), jnp.float32)
    number = []
    for i, c in enumerate(chunks):
        number.append(jnp.where(near[:, c] > 0.0, counts[i : i + 1] + (before - 1.0), -1.0).astype(jnp.int32))
        before = before + counts[i : i + 1, PICK - 1 : PICK]
    total = jnp.sum(near).astype(jnp.int32)

    def slab(start, first):
        picked = jnp.zeros((8, PICK), jnp.float32)
        for i, c in enumerate(chunks):
            chosen = jnp.where(down + start == number[i], 1.0, 0.0).astype(jnp.bfloat16)
            picked = picked + lax.dot_general(
                facts[:, c], chosen, (((1,), (1,)), ((), ())), preferred_element_type=jnp.float32
            )
        px, layer, py = (picked[i : i + 1].astype(jnp.int32) for i in range(3))
        py = py - RAD
        real = picked[3:4] > 0.5
        in_middle = real & (py >= 0) & (py < BY)
        in_rim = real & ((py < RIM) | (py >= BY - RIM))
        rim_lane = jnp.where(py < 0, py + BY, jnp.where(py < RIM, py, py - SHIFT))
        for spot, column, rows, outs in (
            (jnp.where(in_middle, px * NZ + layer, -1), py, NZ, (q_o, h_o)),
            (jnp.where(in_rim, px * NZ + layer, -1), rim_lane, NZ, (q_rim_o, h_rim_o)),
        ):
            there = lax.broadcasted_iota(jnp.int32, (BY, PICK), 0) == column
            for i, out in enumerate(outs):
                parts = [jnp.where(there, picked[4 + 2 * i + j : 5 + 2 * i + j], 0.0).astype(jnp.bfloat16) for j in range(2)]
                for x0, x1 in ((1, 14), (14, 27)) if i == 0 else ((5, 14), (14, 23)):
                    index = lax.broadcasted_iota(jnp.int32, ((x1 - x0) * rows, PICK), 0) + x0 * rows
                    hit = jnp.where(index == spot, 1.0, 0.0).astype(jnp.bfloat16)
                    value = jnp.zeros(((x1 - x0) * rows, BY), jnp.float32)
                    for part in parts:
                        value = value + lax.dot_general(
                            hit, part, (((1,), (1,)), ((), ())), preferred_element_type=jnp.float32
                        )
                    value = value.reshape(x1 - x0, rows, BY)
                    out[x0:x1] = value if first else out[x0:x1] + value

    slab(0, True)

    @pl.loop(1, (total + (PICK - 1)) // PICK)
    def _(i):
        slab(i * PICK, False)


def face(t, pi, pj, ti, tj, di, dj):
    dp = pi - pj
    u = t * dp
    v = u * u + SMOOTH
    inv = lax.rsqrt(v)
    speed = v * inv
    db = 0.5 * (di + dj)
    dt = ti - tj
    st = 0.5 * (ti + tj)
    flux = (CONDUCT + db * speed) * dt + u * st
    e = db * (u * inv) * dt + st
    return flux, e * t, e * dp, speed * dt


def solve(scratch, source, heat, ends, perm_sens, disp_sens):
    (
        K, D, T, O, P0, P1, P2, P3, P4, TX, TY, TZ, R, M, U0, U1, U2, U3, W,
        AX, AY, AZ, AB, BXX, BYY, BZZ, BBB, CXX, CYY, CZZ, CBB,
    ) = scratch
    PR = (P0, P1, P2, P3, P4)
    MU = (U0, U1, U2, U3)
    at = lax.broadcasted_iota(jnp.int32, (NZ, BY), 0)
    top = at == NZ - 1
    bottom = at == 0

    def above(a):
        return jnp.concatenate([a[8:], roll(a[:8], -1, 0)], axis=0)

    def below(a):
        return jnp.concatenate([roll(a[24:], 1, 0), a[:24]], axis=0)

    def ahead(a):
        return roll(a, -1, 1)

    def behind(a):
        return roll(a, 1, 1)

    def coefficients(x, before):
        k = K[x]
        tx = 0.5 * (k + K[x + 1])
        ty = 0.5 * (k + ahead(k))
        half = 0.5 * k
        tz = jnp.where(top, 0.0, half + above(half))
        total = STORAGE + before + tx + ty + behind(ty) + tz + below(tz)
        total = total + jnp.where(top | bottom, half, 0.0)
        TX[x] = tx
        TY[x] = ty
        TZ[x] = tz
        R[x] = jnp.where(k > 0.0, 1.0 / total, 0.0)
        return tx

    TX[0] = 0.5 * (K[0] + K[1])
    lax.fori_loop(1, WX - 1, coefficients, 0.5 * (K[0] + K[1]), unroll=13)

    def spread(ref, x):
        a = ref[x]
        ty, tz = TY[x], TZ[x]
        return (
            TX[x] * ref[x + 1]
            + TX[x - 1] * ref[x - 1]
            + ty * ahead(a)
            + behind(ty * a)
            + tz * above(a)
            + below(tz * a)
        )

    for s in range(1, 5):

        def sweep(x, carry, s=s):
            PR[s][x] = (source[x] + spread(PR[s - 1], x)) * R[x]
            return carry

        lax.fori_loop(s, WX - s, sweep, 0, unroll=True)

    PE = PR[4]

    def face_x(x):
        return face(TX[x], PE[x], PE[x + 1], T[x], T[x + 1], D[x], D[x + 1])

    def transport(keep):
        def step(x, before):
            t, p, d = T[x], PE[x], D[x]
            fx, ax, bx, cx = face_x(x)
            fy, ay, by, cy = face(TY[x], p, ahead(p), t, ahead(t), d, ahead(d))
            half = 0.5 * K[x]
            tz = TZ[x] + jnp.where(top, half, 0.0)

            def over(a):
                return jnp.where(top, 0.0, above(a))

            fz, az, bz, cz = face(tz, p, over(p), t, over(t), d, over(d))
            fb, ab, bb, cb = face(half[0:8], p[0:8], 0.0, t[0:8], 0.0, d[0:8], 0.0)
            fall = jnp.concatenate([-fb, jnp.zeros((NZ - 8, BY), jnp.float32)], axis=0)
            out = fx - before + fy - behind(fy) + fz - jnp.where(bottom, fall, below(fz))
            end = t + TIME_STEP * (HEAT_GAIN * heat[x] - out)
            M[x] = jnp.where(R[x] > 0.0, (-TIME_STEP) * (end - O[x]), 0.0)
            AX[x], AY[x], AZ[x], AB[x] = ax, ay, az, ab
            if keep:
                BXX[x], BYY[x], BZZ[x], BBB[x] = bx, by, bz, bb
                CXX[x], CYY[x], CZZ[x], CBB[x] = cx, cy, cz, cb
                ends[x - 9] = end
            return fx

        return step

    first = face_x(4)[0]
    first = lax.fori_loop(5, 9, transport(False), first, unroll=True)
    first = lax.fori_loop(9, 18, transport(True), first, unroll=3)
    lax.fori_loop(18, 23, transport(False), first, unroll=True)

    def lift(a, b8):
        wide = jnp.concatenate([b8, jnp.zeros((NZ - 8, BY), jnp.float32)], axis=0)
        return jnp.where(bottom, wide, a)

    def pull_press(x, before):
        m = M[x]
        gx = (m - M[x + 1]) * AX[x]
        gy = (m - ahead(m)) * AY[x]
        gz = (m - jnp.where(top, 0.0, above(m))) * AZ[x]
        gb = m[0:8] * AB[x]
        lam = gx - before + gy - behind(gy) + gz + lift(-below(gz), gb)
        MU[3][x] = lam * R[x]
        return gx

    lax.fori_loop(6, 22, pull_press, (M[5] - M[6]) * AX[5], unroll=8)

    for s in range(3, 0, -1):

        def sweep_back(x, carry, s=s):
            MU[s - 1][x] = spread(MU[s], x) * R[x]
            return carry

        lax.fori_loop(10 - s, 18 + s, sweep_back, 0, unroll=True)

    def products(x, carry):
        total = MU[0][x] * PR[1][x]
        for s in range(1, 4):
            total = total + MU[s][x] * PR[s + 1][x]
        W[x] = total
        return carry

    lax.fori_loop(9, 19, products, 0, unroll=True)

    def around(ref, x):
        a = ref[x]
        return (
            ref[x - 1]
            + ref[x + 1]
            + ahead(a)
            + behind(a)
            + jnp.where(top, 0.0, above(a))
            + jnp.where(bottom, 0.0, below(a))
        )

    def sensitivities(x, carry):
        m = M[x]
        gx = m - M[x + 1]
        gw = M[x - 1] - m
        gy = m - ahead(m)
        gz = m - jnp.where(top, 0.0, above(m))
        gb = m[0:8]

        def both(fx, fy, fz, fb):
            ay = gy * fy[x]
            az = gz * fz[x]
            return gx * fx[x] + gw * fx[x - 1] + ay + behind(ay) + az + lift(below(az), gb * fb[x])

        gk = both(BXX, BYY, BZZ, BBB)
        gd = both(CXX, CYY, CZZ, CBB)
        gk = gk - 6.0 * W[x] - around(W, x)
        for s in range(4):
            gk = gk + MU[s][x] * around(PR[s], x) + PR[s][x] * around(MU[s], x)
        perm_sens[x - OWN] = 0.5 * gk * K[x]
        disp_sens[x - OWN] = 0.5 * gd * D[x]
        return carry

    lax.fori_loop(OWN, OWN + BX, sensitivities, 0, unroll=True)


def look(table, i, index):
    wide = jnp.broadcast_to(table[i : i + 1], index.shape)
    return jnp.take_along_axis(wide, index, axis=1, mode="promise_in_bounds")


def middle_kernel(zone, press, temp, seen, up, down, up2, down2, after, source, heat, table, ends, perm_sens, disp_sens, *scratch):
    K, D, T, O, start = scratch[:5]
    for r in range(WX):
        row = grid_row(r, zone, press, temp, seen, up, down, up2, down2)
        z = row["z"].astype(jnp.int32)
        start[r] = row["p"]
        K[r] = look(table, 0, z)
        if 4 <= r < 24:
            D[r] = look(table, 1, z)
            T[r] = row["t"]
        if 5 <= r < 23:
            O[r] = row["o"]

    solve(scratch, source, heat, ends, perm_sens, disp_sens)


def rim_kernel(
    zone, press, temp, seen, up, down, up2, down2, left, right, source, heat, table, mid_ends, mid_perm, mid_disp,
    temp_o, sens_o, sums_o, ends, perm_sens, disp_sens, SP, SD, Z, PART, temp_v, sens_v, sems, *scratch,
):
    K, D, T, O, start = scratch[:5]
    lane = lanes((NZ, BY))

    moved = (lane >= 54) & (lane < 86)
    patterns = {}

    def rims(field, packed, spot, reach):
        part = jnp.where(moved, roll(field, -SHIFT, 1), field)
        if packed is None:
            return part
        if (spot, reach) not in patterns:
            index = (jnp.where(lane < 86, lane - (BY - SHIFT), lane) + spot) & (BY - 1)
            patterns[spot, reach] = index, (lane >= BY - reach) | ((lane >= 76) & (lane < 76 + reach))
        index, here = patterns[spot, reach]
        return jnp.where(here, jnp.take_along_axis(packed, index, axis=1, mode="promise_in_bounds"), part)

    sides = {}
    for r in range(WX):
        row = grid_row(r, zone, press, temp, seen, up, down, up2, down2)
        index, places = edge_place(r)

        if index not in sides:
            sides[index] = left[index] + right[index]

        def both(name, index=index, places=places, row=row):
            return rims(row[name].astype(jnp.float32), sides[index], *places[name])

        start[r] = both("p")
        z = both("z").astype(jnp.int32)
        K[r] = look(table, 0, z)
        if 4 <= r < 24:
            D[r] = look(table, 1, z)
            T[r] = both("t")
        if 5 <= r < 23:
            O[r] = both("o") if "o" in places else rims(row["o"], None, 0, 0)

    solve(scratch, source, heat, ends, perm_sens, disp_sens)

    def joined(middle, rim):
        return jnp.where(lane < RAD, rim, jnp.where(lane >= BY - RAD, roll(rim, SHIFT, 1), middle))

    for x in range(BX):
        put_rows(temp_v, x, joined(mid_ends[x + 1], ends[x + 1]))
        SP[x] = joined(mid_perm[x], perm_sens[x])
        SD[x] = joined(mid_disp[x], disp_sens[x])
        put_rows(sens_v, x, SP[x])
        Z[x] = rows_of(zone, x).astype(jnp.float32)

    copies = [
        pltpu.make_async_copy(temp_v, temp_o, sems.at[0]),
        pltpu.make_async_copy(sens_v, sens_o, sems.at[1]),
    ]
    for copy in copies:
        copy.start()

    def of_zone(z, carry):
        zf = z.astype(jnp.float32)
        total_p = jnp.zeros((NZ, BY), jnp.float32)
        total_d = jnp.zeros((NZ, BY), jnp.float32)
        for x in range(BX):
            here = Z[x] == zf
            total_p = total_p + jnp.where(here, SP[x], 0.0)
            total_d = total_d + jnp.where(here, SD[x], 0.0)
        PART[z] = jnp.sum(total_p.reshape(4, 8, BY), axis=0)
        PART[z + 64] = jnp.sum(total_d.reshape(4, 8, BY), axis=0)
        return carry

    lax.fori_loop(0, 64, of_zone, 0, unroll=16)
    per_lane = jnp.sum(PART[...], axis=1)
    sums_o[...] = lax.dot_general(
        jnp.ones((8, BY), jnp.float32),
        per_lane,
        (((1,), (1,)), ((), ())),
        precision=lax.Precision.HIGHEST,
        preferred_element_type=jnp.float32,
    )
    for copy in copies:
        copy.wait()


def shifted(array, axis, by):
    size = lax.axis_size(axis)
    pairs = [(i, i + by) for i in range(size) if 0 <= i + by < size]
    return lax.ppermute(array, axis, pairs)


def spread_sum(array, axis):
    size = lax.axis_size(axis)
    copies = jnp.broadcast_to(array[None], (size,) + array.shape)
    return lax.all_to_all(copies, axis, 0, 0).sum(0)


def f32(*shape):
    return jax.ShapeDtypeStruct(shape, jnp.float32)


def buf(*shape):
    return pltpu.VMEM(shape, jnp.float32)


SOLVE = [buf(WX, NZ, BY)] * 19 + ([buf(23, NZ, BY)] * 3 + [buf(23, 8, BY)]) * 3


def body(zone_ids, log_perm, log_disp, temp_start, pressure_start, temp_observed, well_cells, well_flow, plan, inject_temp):
    flat = (NZ * BX, BY)
    zone = zone_ids.reshape(flat)
    press = pressure_start.reshape(flat)
    temp = temp_start.reshape(flat)
    seen = temp_observed.reshape(flat)
    grid_rows = BX * lax.axis_size("gx")
    grid_cols = BY * lax.axis_size("gy")

    to_up, to_down, to_up2, to_down2 = pl.pallas_call(
        pack_rows_kernel,
        out_shape=(f32(SIDE, NZ, BY), f32(SIDE, NZ, BY), f32(FAR, NZ, BY), f32(FAR, NZ, BY)),
        in_specs=[VMEM] * 4,
        out_specs=(VMEM,) * 4,
        compiler_params=FULL,
        name="pack_rows",
    )(zone, press, temp, seen)
    up = shifted(to_up, "gx", 1)
    down = shifted(to_down, "gx", -1)
    up2 = shifted(to_up2, "gx", 2)
    down2 = shifted(to_down2, "gx", -2)

    corner = jnp.stack([lax.axis_index("gx") * BX, lax.axis_index("gy") * BY]).astype(jnp.int32)
    source, heat, rim_source, rim_heat, table = pl.pallas_call(
        lambda *refs: wells_kernel(grid_rows, grid_cols, *refs),
        out_shape=(f32(WX, NZ, BY),) * 4 + (f32(8, BY),),
        in_specs=[SMEM] + [VMEM] * 6,
        out_specs=(VMEM,) * 5,
        compiler_params=PARAMS,
        cost_estimate=pl.CostEstimate(flops=1 << 28, bytes_accessed=2 << 20, transcendentals=0),
        name="wells",
    )(corner, well_cells[None], well_flow[None], plan, inject_temp, log_perm[None], log_disp[None])

    to_right, to_left = pl.pallas_call(
        pack_columns_kernel,
        out_shape=(f32(EDGE, NZ, BY), f32(EDGE, NZ, BY)),
        in_specs=[VMEM] * 8 + [pl.BlockSpec(memory_space=pl.ANY)],
        out_specs=(VMEM,) * 2,
        compiler_params=PARAMS,
        name="pack_columns",
    )(zone, press, temp, seen, up, down, up2, down2, table)
    left = shifted(to_right, "gy", 1)
    right = shifted(to_left, "gy", -1)

    own = (f32(9, NZ, BY), f32(BX, NZ, BY), f32(BX, NZ, BY))
    mid_ends, mid_perm, mid_disp = pl.pallas_call(
        middle_kernel,
        out_shape=own,
        in_specs=[VMEM] * 8 + [pl.BlockSpec(memory_space=pl.ANY)] + [VMEM] * 3,
        out_specs=(VMEM,) * 3,
        scratch_shapes=SOLVE,
        compiler_params=PARAMS,
        cost_estimate=pl.CostEstimate(flops=1 << 28, bytes_accessed=4 << 20, transcendentals=0),
        name="middle",
    )(zone, press, temp, seen, up, down, up2, down2, to_right, source, heat, table)
    temp_end, sens, sums = pl.pallas_call(
        rim_kernel,
        out_shape=(f32(*flat), f32(*flat), f32(8, BY)),
        in_specs=[VMEM] * 16,
        out_specs=(pl.BlockSpec(memory_space=pl.ANY), pl.BlockSpec(memory_space=pl.ANY), VMEM),
        scratch_shapes=[buf(9, NZ, BY), buf(BX, NZ, BY), buf(BX, NZ, BY)]
        + [buf(BX, NZ, BY)] * 3
        + [buf(128, 8, BY), buf(*flat), buf(*flat), pltpu.SemaphoreType.DMA((2,))]
        + SOLVE,
        compiler_params=PARAMS,
        name="rims",
    )(
        zone, press, temp, seen, up, down, up2, down2, left, right, rim_source, rim_heat, table,
        mid_ends, mid_perm, mid_disp,
    )

    totals = spread_sum(sums[0:1], ("gx", "season"))
    totals = spread_sum(totals, "gy")
    cells = lax.axis_size("season") * NZ * grid_rows * grid_cols
    gradient = totals.reshape(2, 64) * (cells / 64) ** (-0.5)
    return (temp_end.reshape(temp_start.shape), sens.reshape(temp_start.shape), gradient)


def solution(mesh):
    in_specs = (
        P(None, "gx", "gy"),
        P(),
        P(),
        P("season", None, "gx", "gy"),
        P("season", None, "gx", "gy"),
        P("season", None, "gx", "gy"),
        P(),
        P(),
        P("season", None),
        P("season", None),
    )
    out_specs = (P("season", None, "gx", "gy"), P("season", None, "gx", "gy"), P())
    return jax.shard_map(body, mesh=mesh, in_specs=in_specs, out_specs=out_specs, check_vma=False)
```
